256 devices in a mesh: seq: 8 (over z_hi, x), roll: 32 (over y, z_lo, core).
Axes of the slice: x: 4, y: 4, z: 8 (z_hi: 2, z_lo: 4; z = z_hi * 4 + z_lo), core: 2. Of those that a mesh axis runs over, the one named last changes fastest.
Arguments:
- x_prompt: bfloat16 [2048, 4096], P('seq', 'roll'), may hold values from -6 to 6
- dt_prompt: float32 [64, 2048], P('roll', 'seq'), may hold values from 0.01 to 0.24, as said below
- b_prompt: bfloat16 [2048, 512], P('seq'), may hold values from -1.796875 to 1.796875
- x_roll: bfloat16 [32, 1024, 4096], P('roll', 'seq'), may hold values from -6 to 6
- dt_roll: float32 [32, 64, 1024], P('roll', None, 'seq'), may hold values from 0.01 to 0.24, as said below
- b_roll: bfloat16 [32, 1024, 512], P('roll', 'seq'), may hold values from -1.796875 to 1.796875
- c_roll: bfloat16 [32, 1024, 512], P('roll', 'seq'), may hold values from -1.796875 to 1.796875
- rate: float32 [64], replicated, may hold values from 0.002 to 1, as said below
- skip: float32 [64], replicated, may hold values from 0.1 to 1.9
- grad_y: bfloat16 [32, 1024, 4096], P('roll', 'seq'), may hold values from -6 to 6
- roll_len: int32 [32], P('roll'), may hold values from 256 to 1024
- prompt_len: int32 [1], replicated, may hold values from 1024 to 2048
Outputs:
- grad_x_prompt: bfloat16 [2048, 4096], P('seq', 'roll')
- grad_b_prompt: bfloat16 [2048, 512], P('seq')
- grad_dt_prompt: float32 [64, 2048], P('roll', 'seq')
- grad_x_roll: bfloat16 [32, 1024, 4096], P('roll', 'seq')
- grad_b_roll: bfloat16 [32, 1024, 512], P('roll', 'seq')
- grad_c_roll: bfloat16 [32, 1024, 512], P('roll', 'seq')
- grad_dt_roll: float32 [32, 64, 1024], P('roll', None, 'seq')
The draws below stay inside these ranges and needn't reach their ends.
Inputs may be any that keep to these rules, and one draw needn't show every extreme that they name: `dt_prompt`: positive step sizes. `dt_roll`: positive step sizes. `rate`: positive rates.
All inputs are finite; a program needn't handle non-finite values.
Results may differ from the reference program's by a relative error of at most 0.012.
Values may be sent and summed in bfloat16 or wider, within the bound.
A program may use at most 128 MiB of HBM per device.

```python
import math
import jax
import jax.numpy as jnp
from jax import lax

HEADS = 64
HEAD_DIM = 64
STATE = 128
GROUPS = 4
PR_DEV = 256
RL_DEV = 128
PROMPT = 2048
RLEN = 1024
ROLLOUTS = 32


def log_range(key, shape, low, high):
    return jnp.exp(jax.random.uniform(key, shape, jnp.float32, jnp.log(low), jnp.log(high)))


def step_field(key, shape, span, low, high):
    base_key, block_key = jax.random.split(key)
    base = log_range(base_key, shape, low, high)
    factors = log_range(block_key, shape[:-1] + (shape[-1] // span,), 0.5, 2.0)
    return base * jnp.repeat(factors, span, axis=-1)


def draw_rate(key, part):
    key = jax.random.fold_in(key, 11)
    pick_key, slow_key, fast_key = jax.random.split(key, 3)
    slow_share = 0.5
    slow_heads = jax.random.uniform(pick_key, (HEADS,)) < slow_share
    return jnp.where(slow_heads, log_range(slow_key, (HEADS,), 0.002, 0.01), log_range(fast_key, (HEADS,), 0.3, 1.0))


def draw_dt_prompt(key, part):
    key = jax.random.fold_in(key, 12)
    return step_field(key, (HEADS, PROMPT), PR_DEV, 0.02, 0.12)


def draw_dt_roll(key, part):
    key = jax.random.fold_in(key, 13)
    return step_field(key, (ROLLOUTS, HEADS, RLEN), RL_DEV, 0.02, 0.12)


def touch_ends(drawn, rng, least, largest):
    longest = drawn.shape.index(max(drawn.shape))
    spots = []
    for shift in (0, 1):
        where = [jax.random.randint(jax.random.fold_in(rng, axis), (), 0, length) for axis, length in enumerate(drawn.shape)]
        where[longest] = (where[longest] + shift) % drawn.shape[longest]
        spots.append(tuple(where))
    return drawn.at[spots[0]].set(least).at[spots[1]].set(largest)


def steps_of(rng, shape, pieces, smallest, largest):
    level = 1.0
    for position, parts in pieces:
        draws = jax.random.uniform(jax.random.fold_in(jax.random.fold_in(rng, 6), position), (parts,), jnp.float32, smallest / len(pieces), largest / len(pieces))
        level = level * jnp.repeat(jnp.exp(draws), shape[position] // parts).reshape((-1,) + (1,) * (len(shape) - 1 - position))
    return level


def centred(own_key, shape, deviation, reach, cuts=(), held_as=jnp.bfloat16):
    level = steps_of(own_key, shape, cuts, -0.22, 0.18) if cuts else 1.0
    drawn = jax.random.normal(own_key, shape, jnp.float32) * deviation * level
    return jnp.minimum(jnp.maximum(drawn, -reach), reach).astype(held_as)


def setup_inputs(seed: int = 0) -> dict:
    key_list = jax.random.split(jax.random.key(seed), 13)
    return {
        "x_prompt": centred(key_list[0], (PROMPT, HEADS * HEAD_DIM), 1.0, 6.0, ((0, 8), (1, 32))),
        "dt_prompt": draw_dt_prompt(jax.random.fold_in(key_list[12], 71), 0),
        "b_prompt": centred(key_list[2], (PROMPT, GROUPS * STATE), 0.3, 1.796875, ((0, 8),)),
        "x_roll": centred(key_list[3], (ROLLOUTS, RLEN, HEADS * HEAD_DIM), 1.0, 6.0, ((0, 32), (1, 8))),
        "dt_roll": draw_dt_roll(jax.random.fold_in(key_list[12], 71), 0),
        "b_roll": centred(key_list[5], (ROLLOUTS, RLEN, GROUPS * STATE), 0.3, 1.796875, ((0, 32), (1, 8))),
        "c_roll": centred(key_list[6], (ROLLOUTS, RLEN, GROUPS * STATE), 0.3, 1.796875, ((0, 32), (1, 8))),
        "rate": draw_rate(jax.random.fold_in(key_list[12], 71), 0),
        "skip": jnp.clip(1.0 + 0.18 * jax.random.normal(key_list[8], (HEADS,), jnp.float32), 0.1, 1.9),
        "grad_y": centred(key_list[9], (ROLLOUTS, RLEN, HEADS * HEAD_DIM), 1.0, 6.0, ((0, 32), (1, 8))),
        "roll_len": touch_ends(jax.random.randint(key_list[10], (ROLLOUTS,), RLEN // 4, RLEN + 1), jax.random.fold_in(key_list[10], 1), RLEN // 4, RLEN).astype(jnp.int32),
        "prompt_len": jax.random.randint(key_list[11], (1,), PROMPT // 2, PROMPT + 1).astype(jnp.int32),
    }


def exact_product(spec, *operands):
    return jnp.einsum(spec, *[operand.astype(jnp.float32) for operand in operands], precision=lax.Precision.HIGHEST)


def lead_groups(array_in, groups):
    return array_in.reshape((groups, array_in.shape[0] // groups) + array_in.shape[1:])


def token_groups(array_in, groups):
    return array_in.reshape((array_in.shape[0], groups, array_in.shape[1] // groups) + array_in.shape[2:])


def local_forward(inputs, b_rows, step_rows, log_decay):
    groups = b_rows.shape[1]
    cumulative = jnp.cumsum(log_decay, axis=1)
    weights = jnp.exp(cumulative[:, -1:] - cumulative) * step_rows
    state = exact_product("gkt,tgkp,tgn->gkpn", lead_groups(weights, groups), token_groups(inputs, groups), b_rows)
    return jnp.exp(cumulative[:, -1]), state.reshape(log_decay.shape[0], inputs.shape[2], b_rows.shape[2])


def block_terms(inputs, cotangent, b_rows, c_rows, step_rows, log_decay, rate, skip, live, entry_state, beyond_grad):
    groups = b_rows.shape[1]
    length = inputs.shape[0]
    head_count = log_decay.shape[0]
    per_group = head_count // groups
    cumulative = jnp.cumsum(log_decay, axis=1)
    end_log = cumulative[:, -1:]
    causal_mask = jnp.arange(length)[:, None] >= jnp.arange(length)[None, :]
    gaps = cumulative[:, :, None] - cumulative[:, None, :]
    segment = jnp.where(causal_mask, jnp.exp(jnp.where(causal_mask, gaps, 0.0)), 0.0)
    intersection_cb = exact_product("vgn,ugn->gvu", c_rows, b_rows)
    intersection_gx = exact_product("vhp,uhp->hvu", cotangent, inputs)
    weighted = segment * intersection_gx
    intersection_heads = jnp.repeat(intersection_cb, per_group, axis=0)
    paired = weighted * intersection_heads * step_rows[:, None, :]
    pooled = jnp.sum((weighted * step_rows[:, None, :]).reshape(groups, per_group, length, length), axis=1)
    tail_decay = jnp.exp(end_log - cumulative)
    beyond_groups = lead_groups(beyond_grad, groups)
    pulled = exact_product("tgn,gkpn->tgkp", b_rows, beyond_groups).reshape(length, head_count, -1)
    slope = exact_product("hvu,vhp->uhp", segment * intersection_heads, cotangent) + tail_decay.T[:, :, None] * pulled
    inputs_wide = inputs.astype(jnp.float32)
    grad_inputs = step_rows.T[:, :, None] * slope + skip[None, :, None] * cotangent.astype(jnp.float32)
    outer_weight = (step_rows * tail_decay).T
    grad_b = exact_product("gvu,vgn->ugn", pooled, c_rows) + exact_product(
        "tgkp,gkpn->tgn", token_groups(inputs_wide * outer_weight[:, :, None], groups), beyond_groups)
    seen = exact_product("tgkp,gkpn->tgkn", token_groups(cotangent, groups), lead_groups(entry_state, groups))
    rising = jnp.exp(cumulative).T
    grad_c = exact_product("gvu,ugn->vgn", pooled, b_rows) + jnp.sum(seen * token_groups(rising, groups)[..., None], axis=2)
    entry_terms = rising * jnp.sum(seen * c_rows[:, :, None, :].astype(jnp.float32), axis=3).reshape(length, head_count)
    leave_terms = outer_weight * jnp.sum(inputs_wide * pulled, axis=2)
    carried = jnp.sum(leave_terms, axis=0) + jnp.exp(end_log[:, 0]) * jnp.sum(beyond_grad * entry_state, axis=(1, 2))
    final_slot = (jnp.arange(length) == length - 1).astype(jnp.float32)
    slopes_log = jnp.sum(paired, axis=2) - jnp.sum(paired, axis=1) + (entry_terms - leave_terms).T + carried[:, None] * final_slot[None, :]
    grad_log = lax.cumsum(slopes_log, axis=1, reverse=True)
    grad_step = live[None, :] * (jnp.sum(inputs_wide * slope, axis=2).T - rate[:, None] * grad_log)
    summary = exact_product("gkt,tgkp,tgn->gkpn", lead_groups(rising.T, groups), token_groups(cotangent, groups), c_rows).reshape(beyond_grad.shape)
    backward_state = summary + jnp.exp(end_log)[:, :, None] * beyond_grad
    return grad_inputs, grad_b, grad_c, grad_step, backward_state


def take_rows(array_in, block_index, size):
    return lax.dynamic_slice_in_dim(array_in, block_index.astype(jnp.int32) * size, size, 0)


def take_columns(array_in, block_index, size):
    return lax.dynamic_slice_in_dim(array_in, block_index.astype(jnp.int32) * size, size, 1)


def reference(x_prompt, dt_prompt, b_prompt, x_roll, dt_roll, b_roll, c_roll, rate, skip, grad_y, roll_len, prompt_len):
    size_p = math.gcd(256, PROMPT)
    size_r = math.gcd(256, RLEN)
    blocks_p = PROMPT // size_p
    blocks_r = RLEN // size_r
    live_p = (jnp.arange(PROMPT) >= PROMPT - prompt_len[0]).astype(jnp.float32)
    step_p = dt_prompt * live_p[None, :]
    logd_p = -rate[:, None] * step_p
    inputs_p = x_prompt.reshape(PROMPT, HEADS, HEAD_DIM)
    b_rows_p = b_prompt.reshape(PROMPT, GROUPS, STATE)
    zero_state = jnp.zeros((HEADS, HEAD_DIM, STATE), jnp.float32)

    def prompt_forward(state, block_index):
        decay, local = local_forward(take_rows(inputs_p, block_index, size_p), take_rows(b_rows_p, block_index, size_p),
                                     take_columns(step_p, block_index, size_p), take_columns(logd_p, block_index, size_p))
        return decay[:, None, None] * state + local, state

    fork, enters_p = lax.scan(prompt_forward, zero_state, jnp.arange(blocks_p))

    def one_rollout(pooled_grad, rollout):
        inputs_r = x_roll[rollout].reshape(RLEN, HEADS, HEAD_DIM)
        b_rows_r = b_roll[rollout].reshape(RLEN, GROUPS, STATE)
        c_rows_r = c_roll[rollout].reshape(RLEN, GROUPS, STATE)
        live_mask = jnp.arange(RLEN) < roll_len[rollout]
        live_r = live_mask.astype(jnp.float32)
        cotangent = jnp.where(live_mask[:, None, None], grad_y[rollout].reshape(RLEN, HEADS, HEAD_DIM), jnp.zeros((), jnp.bfloat16))
        step_r = dt_roll[rollout] * live_r[None, :]
        logd_r = -rate[:, None] * step_r

        def forward(state, block_index):
            decay, local = local_forward(take_rows(inputs_r, block_index, size_r), take_rows(b_rows_r, block_index, size_r),
                                         take_columns(step_r, block_index, size_r), take_columns(logd_r, block_index, size_r))
            return decay[:, None, None] * state + local, state

        _, enters_r = lax.scan(forward, fork, jnp.arange(blocks_r))

        def backward(beyond, block_index):
            grad_inputs, grad_b, grad_c, grad_step, back = block_terms(
                take_rows(inputs_r, block_index, size_r), take_rows(cotangent, block_index, size_r),
                take_rows(b_rows_r, block_index, size_r), take_rows(c_rows_r, block_index, size_r),
                take_columns(step_r, block_index, size_r), take_columns(logd_r, block_index, size_r),
                rate, skip, take_rows(live_r, block_index, size_r), enters_r[block_index], beyond)
            return back, (grad_inputs, grad_b, grad_c, grad_step)

        back, (grad_inputs, grad_b, grad_c, grad_step) = lax.scan(backward, zero_state, jnp.arange(blocks_r), reverse=True)
        outputs = (grad_inputs.reshape(RLEN, HEADS * HEAD_DIM).astype(jnp.bfloat16),
                   grad_b.reshape(RLEN, GROUPS * STATE).astype(jnp.bfloat16),
                   grad_c.reshape(RLEN, GROUPS * STATE).astype(jnp.bfloat16),
                   grad_step.transpose(1, 0, 2).reshape(HEADS, RLEN))
        return pooled_grad + back, outputs

    fork_grad, (grad_x_roll, grad_b_roll, grad_c_roll, grad_dt_roll) = lax.scan(one_rollout, zero_state, jnp.arange(ROLLOUTS))
    zero_cot = jnp.zeros((size_p, HEADS, HEAD_DIM), jnp.bfloat16)
    zero_out = jnp.zeros((size_p, GROUPS, STATE), jnp.bfloat16)

    def prompt_backward(beyond, block_index):
        grad_inputs, grad_b, _, grad_step, back = block_terms(
            take_rows(inputs_p, block_index, size_p), zero_cot, take_rows(b_rows_p, block_index, size_p), zero_out,
            take_columns(step_p, block_index, size_p), take_columns(logd_p, block_index, size_p),
            rate, skip, take_rows(live_p, block_index, size_p), enters_p[block_index], beyond)
        return back, (grad_inputs, grad_b, grad_step)

    _, (grad_inputs_p, grad_b_p, grad_step_p) = lax.scan(prompt_backward, fork_grad, jnp.arange(blocks_p), reverse=True)
    return (grad_inputs_p.reshape(PROMPT, HEADS * HEAD_DIM).astype(jnp.bfloat16),
            grad_b_p.reshape(PROMPT, GROUPS * STATE).astype(jnp.bfloat16),
            grad_step_p.transpose(1, 0, 2).reshape(HEADS, PROMPT),
            grad_x_roll, grad_b_roll, grad_c_roll, grad_dt_roll)
```

```python
import functools

import jax
import jax.numpy as jnp
from jax import lax
from jax.experimental import pallas as pl
from jax.experimental.pallas import tpu as pltpu
from jax.sharding import PartitionSpec as P

MESH = pl.DeviceIdType.MESH
F32 = jnp.float32
BF16 = jnp.bfloat16
HEADS = 64
GROUPS = 4
TOK = 128
PTOK = 256
LANE = 128
PAIRS = 32
PER = 8
ROWS = 1024
EXACT = lax.Precision.HIGHEST


def iota(shape, axis):
    return lax.broadcasted_iota(jnp.int32, shape, axis)


def mm(a, b):
    return lax.dot_general(a, b, (((1,), (0,)), ((), ())), preferred_element_type=F32)


def mm_nt(a, b):
    return lax.dot_general(a, b, (((1,), (1,)), ((), ())), preferred_element_type=F32)


def mm_tn(a, b):
    return lax.dot_general(a, b, (((0,), (0,)), ((), ())), preferred_element_type=F32)


def exact(a, b):
    return lax.dot_general(a, b, (((1,), (0,)), ((), ())), preferred_element_type=F32, precision=EXACT)


def halves(value):
    high = value.astype(BF16)
    return high, (value - high.astype(F32)).astype(BF16)


def columns(first, second, rows, length):
    stacked = jnp.where(iota((rows, length), 0) < 64, first, second)
    return stacked.T


def kernel(
    xp_ref, dtp_ref, bp_ref, x_ref, dt_ref, b_ref, c_ref, rate_ref, skip_ref, gy_ref, len_ref, plen_ref,
    gxp_ref, gbp_ref, gdtp_ref, gx_ref, gb_ref, gc_ref, gdt_ref,
    cum, wrow, step, decay, cot, xw, cw, wx, cb, pooled, dxi, zs, xs, car,
    s_loc, l_loc, s_all, l_all, dec_all, t_out, t_in, e_out, b_out, e_all, b_all,
    p_all, pdec, pdec_all, fork_out, fork_all, enter_p, xw_p, wx_p,
    back, fg_all, fg_out, q_all, gbo, gb_all, go_out, go_all,
    ss_p, rs_p, ss_pd, rs_pd, ss_d, rs_d, ss_s, rs_s, ss_l, rs_l, ss_z, rs_z,
    ss_f, rs_f, ss_b, rs_b, ss_e, rs_e, ss_g, rs_g, ss_q, rs_q, ss_gb, rs_gb, ss_go, rs_go,
):
    s = lax.axis_index("seq")
    r = lax.axis_index("roll")
    z, x = s // 4, s % 4
    y, q = r // 8, r % 8

    def at(seq, roll):
        return {"seq": seq, "roll": roll}

    def copy(src, dst, send, recv, seq, roll):
        return pltpu.make_async_remote_copy(
            src_ref=src, dst_ref=dst, send_sem=send, recv_sem=recv, device_id=at(seq, roll), device_id_type=MESH
        )

    bar = pltpu.get_barrier_semaphore()

    def greet(seq, roll):
        pl.semaphore_signal(bar, inc=1, device_id=at(seq, roll), device_id_type=MESH)

    def greet_plane(d, carry):
        greet(s, lax.rem(r + d, 32))
        return carry

    def greet_seq(d, carry):
        greet(lax.rem(s + d, 8), r)
        return carry

    lax.fori_loop(1, 8, greet_seq, 0)
    lax.fori_loop(1, 32, greet_plane, 0)

    def greet_quarter(k, carry):
        @pl.when(jnp.logical_not((s == y) & (k == y)))
        def _():
            greet(y, k * 8 + q)

        return carry

    lax.fori_loop(0, 4, greet_quarter, 0)

    live = (s * TOK + iota((1, TOK), 1) < len_ref[0]).astype(F32)
    step[...] = dt_ref[...] * live
    logd = -rate_ref[...] * step[...]
    upto = (iota((TOK, TOK), 0) <= iota((TOK, TOK), 1)).astype(F32)
    cum_v = exact(logd, upto)
    end_v = exact(logd, jnp.ones((TOK, TOK), F32))
    cum[...] = cum_v
    decay[...] = jnp.exp(end_v)
    wrow[...] = step[...] * jnp.exp(end_v - cum_v)

    low8 = iota((8, PTOK), 0) < 1
    dtp = jnp.where(low8, dtp_ref[0:1, :], dtp_ref[1:2, :])
    r0 = rate_ref[pl.ds(2 * r, 1), :]
    r1 = rate_ref[pl.ds(2 * r + 1, 1), :]
    ratep = jnp.where(low8, jnp.concatenate([r0, r0], axis=1), jnp.concatenate([r1, r1], axis=1))
    first_live = 8 * PTOK - plen_ref[0]
    live_p = (s * PTOK + iota((1, PTOK), 1) >= first_live).astype(F32)
    step_p = dtp * live_p
    logd_p = -ratep * step_p
    upto_p = (iota((PTOK, PTOK), 0) <= iota((PTOK, PTOK), 1)).astype(F32)
    cum_p = exact(logd_p, upto_p)
    end_p = exact(logd_p, jnp.ones((PTOK, PTOK), F32))
    w_p = step_p * jnp.exp(end_p - cum_p)
    pdec[...] = jnp.exp(end_p[:, 0:LANE])
    wx_p[...] = columns(w_p[0:1, :], w_p[1:2, :], LANE, PTOK)
    xw_p[...] = (xp_ref[...].astype(F32) * wx_p[...]).astype(BF16)
    bp = bp_ref[:, pl.ds(pl.multiple_of(y * LANE, LANE), LANE)]
    p_all[s] = mm_tn(xw_p[...], bp).astype(BF16)
    pdec_all[s] = pdec[...]

    extra = jnp.where(z == 0, 8 - (y == x).astype(jnp.int32), 0)
    pl.semaphore_wait(bar, 38 + extra)

    def p_copy(d):
        return copy(p_all.at[s], p_all.at[s], ss_p.at[d], rs_p.at[s], lax.rem(s + d, 8), r)

    def pd_copy(d):
        return copy(pdec, pdec_all.at[s], ss_pd.at[d], rs_pd.at[s], lax.rem(s + d, 8), r)

    def d_copy(d):
        k = lax.rem(x + d, 4)
        return copy(decay.at[pl.ds(pl.multiple_of(k * 16, 16), 16)], dec_all.at[x], ss_d.at[d], rs_d.at[x], z * 4 + k, r)

    def slice_of(k):
        return pl.ds(pl.multiple_of(k * ROWS, ROWS), ROWS)

    def s_copy(d):
        k = lax.rem(x + d, 4)
        return copy(s_loc.at[slice_of(k)], s_all.at[x], ss_s.at[d], rs_s.at[x], z * 4 + k, r)

    def l_copy(d):
        k = lax.rem(x + d, 4)
        return copy(l_loc.at[slice_of(k)], l_all.at[x], ss_l.at[d], rs_l.at[x], z * 4 + k, r)

    def z_copy():
        return copy(t_out, t_in, ss_z, rs_z, (1 - z) * 4 + x, r)

    def f_copy(d):
        return copy(fork_out, fork_all.at[q], ss_f.at[d], rs_f.at[q], s, lax.rem(r + d, 32))

    def b_copy(d):
        k = lax.rem(x + d, 4)
        return copy(b_out.at[k], b_all.at[slice_of(x)], ss_b.at[d], rs_b.at[x], z * 4 + k, r)

    def e_copy(d):
        k = lax.rem(x + d, 4)
        return copy(e_out.at[k], e_all.at[slice_of(x)], ss_e.at[d], rs_e.at[x], z * 4 + k, r)

    def g_copy(d):
        t = lax.rem(r + d, 32)
        piece = pl.multiple_of(lax.rem(t, 8) * 128 + t // 8 * 32, 32)
        return copy(back.at[pl.ds(piece, 32)], fg_all.at[r], ss_g.at[d], rs_g.at[r], s, t)

    def q_copy(k):
        return copy(fg_out, q_all.at[y], ss_q.at[k], rs_q.at[y], k, x * 8 + q)

    def gb_copy(d):
        t = lax.rem(q + d, 8)
        return copy(gbo.at[pl.ds(pl.multiple_of(t * 32, 32), 32)], gb_all.at[q], ss_gb.at[d], rs_gb.at[q], s, y * 8 + t)

    def go_copy(d):
        return copy(go_out, go_all.at[r], ss_go.at[d], rs_go.at[r], s, lax.rem(r + d, 32))

    def each(first, last, act):
        def body(d, carry):
            act(d)
            return carry

        lax.fori_loop(first, last, body, 0)

    each(1, 8, lambda d: p_copy(d).start())
    each(1, 8, lambda d: pd_copy(d).start())
    each(1, 4, lambda d: d_copy(d).start())
    dec_all[x] = decay[pl.ds(pl.multiple_of(x * 16, 16), 16), :]

    row_live = iota((TOK, LANE), 0) + s * TOK < len_ref[0]

    def lanes(i):
        return pl.ds(pl.multiple_of(i * LANE, LANE), LANE)

    def s_pair(i, c_g):
        cx = columns(cum[pl.ds(2 * i, 1), :], cum[pl.ds(2 * i + 1, 1), :], LANE, TOK)
        ct = jnp.where(row_live, gy_ref[:, lanes(i)].astype(F32), 0.0)
        cot[:, lanes(i)] = ct.astype(BF16)
        weighted = (ct * jnp.exp(cx)).astype(BF16)
        cw[:, lanes(i)] = weighted
        s_loc[lanes(i), :] = mm_tn(weighted, c_g).astype(BF16)

    def l_pair(i, b_g):
        wide = columns(wrow[pl.ds(2 * i, 1), :], wrow[pl.ds(2 * i + 1, 1), :], LANE, TOK)
        wx[:, lanes(i)] = wide
        weighted = (x_ref[:, lanes(i)].astype(F32) * wide).astype(BF16)
        xw[:, lanes(i)] = weighted
        l_loc[lanes(i), :] = mm_tn(weighted, b_g).astype(BF16)

    for d in (2, 1, 3, 0):
        g = lax.rem(x + d, 4)
        c_g = c_ref[:, lanes(g)]
        each(0, PER, lambda i: s_pair(g * PER + i, c_g))
        if d:
            s_copy(d).start()
        else:
            s_all[x] = s_loc[slice_of(x), :]
    for d in (2, 1, 3, 0):
        g = lax.rem(x + d, 4)
        b_g = b_ref[:, lanes(g)]
        each(0, PER, lambda i: l_pair(g * PER + i, b_g))
        if d:
            l_copy(d).start()
        else:
            l_all[x] = l_loc[slice_of(x), :]

    def wait_from(count, mine, make):
        def body(d, carry):
            make(lax.rem(mine + d, count)).wait_recv()
            return carry

        lax.fori_loop(1, count, body, 0)

    wait_from(8, s, lambda k: copy(p_all.at[k], p_all.at[k], ss_p.at[0], rs_p.at[k], s, r))
    wait_from(8, s, lambda k: copy(pdec, pdec_all.at[k], ss_pd.at[0], rs_pd.at[k], s, r))
    top = iota((LANE, LANE), 0) < 64

    zero = jnp.zeros((LANE, LANE), F32)
    enter_p[...] = zero
    fork = p_all[0].astype(F32)
    for k in range(1, 8):
        enter_p[...] = jnp.where(k == s, fork, enter_p[...])
        fork = jnp.where(top, pdec_all[k, 0:1, :], pdec_all[k, 1:2, :]) * fork + p_all[k].astype(F32)

    @pl.when((z == 0) & (y == x))
    def _():
        fork_out[...] = fork.astype(BF16)
        fork_all[q] = fork.astype(BF16)
        each(1, 32, lambda d: f_copy(d).start())

    for g in range(GROUPS):
        cb[g] = mm_nt(c_ref[:, g * LANE : (g + 1) * LANE], b_ref[:, g * LANE : (g + 1) * LANE])
        pooled[g] = zero
    zs[...] = jnp.zeros_like(zs)
    xs[...] = jnp.zeros_like(xs)
    car[...] = jnp.zeros_like(car)
    causal = iota((TOK, TOK), 0) >= iota((TOK, TOK), 1)
    left = iota((TOK, LANE), 1) < 64

    def collect(i, zz, xd):
        z_hi, z_lo = halves(zz)
        row = iota((16, 3 * LANE), 0)
        lane = iota((16, 3 * LANE), 1)
        slot = 2 * lax.rem(i, 4) + (lax.rem(lane, LANE) >= 64).astype(jnp.int32)
        slot = slot + jnp.where(lane >= 2 * LANE, 8, 0)
        pick = (row == slot).astype(F32).astype(BF16)
        sums = mm_nt(pick, jnp.concatenate([z_hi, z_lo, xd.astype(BF16)], axis=1))
        at8 = pl.ds(pl.multiple_of(i // 4 * 8, 8), 8)
        zs[at8, :] = zs[at8, :] + sums[0:8]
        xs[at8, :] = xs[at8, :] + sums[8:16]

    def intra(i):
        g = i // PER
        xi = x_ref[:, lanes(i)]
        ci = cot[:, lanes(i)]
        xf = xi.astype(F32)
        cf = ci.astype(F32)
        both = jnp.concatenate([jnp.where(left, cf, 0.0).astype(BF16), jnp.where(left, 0.0, cf).astype(BF16)], axis=0)
        gx = mm_nt(both, xi)
        cbg = cb[g]
        mixes = []
        total = pooled[g]
        for a in range(2):
            row = cum[pl.ds(2 * i + a, 1), :]
            col = jnp.broadcast_to(row, (TOK, TOK)).T
            seg = jnp.where(causal, jnp.exp(col - row), 0.0) * step[pl.ds(2 * i + a, 1), :]
            total = total + seg * gx[a * TOK : (a + 1) * TOK]
            mixes.append((seg * cbg).astype(BF16))
        pooled[g] = total
        mix = jnp.concatenate(mixes, axis=0)
        dx = mm_tn(mix, both)
        yy = mm(mix, xi)
        yi = jnp.where(left, yy[:TOK], yy[TOK:])
        dxi[:, lanes(i)] = dx
        xd = xf * dx
        collect(i, cf * yi - xd, xd)

    each(0, PAIRS // 2, intra)

    wait_from(4, x, lambda k: copy(decay.at[pl.ds(0, 16)], dec_all.at[k], ss_d.at[0], rs_d.at[k], s, r))
    wait_from(4, x, lambda k: copy(s_all.at[k], s_all.at[k], ss_s.at[0], rs_s.at[k], s, r))

    def head_rows(h):
        return pl.ds(pl.multiple_of(h * 64, 64), 64)

    def backward(start, finish):
        def body(h):
            state = start(head_rows(h))
            for k in (3, 2, 1, 0):
                b_out[k, head_rows(h), :] = state.astype(BF16)
                state = dec_all[k, pl.ds(h, 1), :] * state + s_all[k, head_rows(h), :].astype(F32)
            finish[head_rows(h), :] = state.astype(BF16)

        each(0, 16, body)

    def forward(start, finish):
        def body(h):
            state = start(head_rows(h))
            for k in range(4):
                e_out[k, head_rows(h), :] = state.astype(BF16)
                state = dec_all[k, pl.ds(h, 1), :] * state + l_all[k, head_rows(h), :].astype(F32)
            if finish is not None:
                finish[head_rows(h), :] = state.astype(BF16)

        each(0, 16, body)

    def give_back(out, whole, make):
        for d in (2, 1, 3):
            make(d).start()
        whole[slice_of(x), :] = out[x]

    @pl.when(z == 1)
    def _():
        backward(lambda rows: jnp.zeros((64, LANE), F32), t_out)
        z_copy().start()
        give_back(b_out, b_all, b_copy)

    each(PAIRS // 2, PAIRS, intra)

    wait_from(4, x, lambda k: copy(l_all.at[k], l_all.at[k], ss_l.at[0], rs_l.at[k], s, r))

    @pl.when(z == 0)
    def _():
        def fork_wait(k):
            @pl.when(jnp.logical_not((y == x) & (q == k)))
            def _():
                copy(fork_out, fork_all.at[k], ss_f.at[0], rs_f.at[k], s, r).wait_recv()

        each(0, 8, fork_wait)

        def body(h):
            state = fork_all[h // 2, pl.ds(pl.multiple_of(lax.rem(h, 2) * 64, 64), 64), :].astype(F32)
            for k in range(4):
                e_out[k, head_rows(h), :] = state.astype(BF16)
                state = dec_all[k, pl.ds(h, 1), :] * state + l_all[k, head_rows(h), :].astype(F32)
            t_out[head_rows(h), :] = state.astype(BF16)

        each(0, 16, body)
        z_copy().start()
        z_copy().wait_recv()
        backward(lambda rows: t_in[rows, :].astype(F32), back)
        each(1, 32, lambda d: g_copy(d).start())
        own = pl.multiple_of(q * 128 + y * 32, 32)
        fg_all[r] = back[pl.ds(own, 32), :]
        give_back(b_out, b_all, b_copy)
        give_back(e_out, e_all, e_copy)

    @pl.when(z == 1)
    def _():
        z_copy().wait_recv()
        forward(lambda rows: t_in[rows, :].astype(F32), None)
        give_back(e_out, e_all, e_copy)

    @pl.when(z == 0)
    def _():
        wait_from(32, r, lambda k: copy(fg_all.at[k], fg_all.at[k], ss_g.at[0], rs_g.at[k], s, r))
        total = fg_all[0].astype(F32)
        for k in range(1, 32):
            total = total + fg_all[k].astype(F32)
        fg_out[...] = total

        def q_send(k):
            @pl.when(jnp.logical_not((k == s) & (y == x)))
            def _():
                q_copy(k).start()

        each(0, 8, q_send)

        @pl.when(y == x)
        def _():
            q_all[y] = total

    def part_b(d):
        g = lax.rem(x + d, 4)
        if d:
            copy(b_out.at[0], b_all.at[slice_of(g)], ss_b.at[0], rs_b.at[g], s, r).wait_recv()
        b_g = b_ref[:, lanes(g)]
        wide = pl.ds(pl.multiple_of(g * ROWS, ROWS), ROWS)

        def pair(j):
            i = g * PER + j
            pulled = mm_nt(b_g, b_all[lanes(i), :])
            inter = wx[:, lanes(i)] * pulled
            xd = x_ref[:, lanes(i)].astype(F32) * inter
            grad = dxi[:, lanes(i)] + inter + skip_ref[:, lanes(i)] * cot[:, lanes(i)].astype(F32)
            gx_ref[:, lanes(i)] = grad.astype(BF16)
            collect(i, -xd, xd)
            leave = jnp.sum(xd, axis=0, keepdims=True)
            row = iota((8, LANE), 0)
            slot = 2 * lax.rem(i, 4) + (iota((8, LANE), 1) >= 64).astype(jnp.int32)
            at8 = pl.ds(pl.multiple_of(i // 4 * 8, 8), 8)
            car[at8, :] = car[at8, :] + jnp.where(row == slot, leave, 0.0)

        each(0, PER, pair)
        grad_b = mm_tn(pooled[g].astype(BF16), c_ref[:, lanes(g)]) + mm(xw[:, wide], b_all[wide, :])
        gb_ref[:, lanes(g)] = grad_b.astype(BF16)

    for d in (0, 1, 3, 2):
        part_b(d)

    def q_wait(k):
        @pl.when(jnp.logical_not((s == y) & (k == y)))
        def _():
            copy(fg_out, q_all.at[k], ss_q.at[0], rs_q.at[k], s, r).wait_recv()

    each(0, 4, q_wait)

    q_whole = jnp.concatenate([q_all[k] for k in range(4)], axis=0)
    for k in range(1, 8):
        q_whole = q_whole * jnp.where(k > s, jnp.where(top, pdec_all[k, 0:1, :], pdec_all[k, 1:2, :]), 1.0)
    q_state = q_whole.astype(BF16)
    pulled_p = mm_nt(bp, q_state)
    dx_p = wx_p[...] * pulled_p
    gxp_ref[...] = dx_p.astype(BF16)
    gbo[...] = mm(xw_p[...], q_state).astype(BF16)
    each(1, 8, lambda d: gb_copy(d).start())
    gb_all[q] = gbo[pl.ds(pl.multiple_of(q * 32, 32), 32), :]
    xd_p = xp_ref[...].astype(F32) * dx_p
    xd_hi, xd_lo = halves(xd_p)
    pick = (iota((8, 2 * LANE), 0) == (lax.rem(iota((8, 2 * LANE), 1), LANE) >= 64).astype(jnp.int32)).astype(F32)
    leave_p = mm_nt(pick.astype(BF16), jnp.concatenate([xd_hi, xd_lo], axis=1))
    before = (iota((PTOK, PTOK), 0) < iota((PTOK, PTOK), 1)).astype(F32)
    passed = exact(leave_p, before)
    meet = q_state.astype(F32) * enter_p[...]
    meet = jnp.where(
        iota((8, LANE), 0) < 1,
        jnp.sum(jnp.where(top, meet, 0.0), axis=0, keepdims=True),
        jnp.sum(jnp.where(top, 0.0, meet), axis=0, keepdims=True),
    )
    through = jnp.sum(meet * pdec[...], axis=1, keepdims=True)
    grad_p = live_p * (leave_p / dtp - ratep * (passed + through))
    gdtp_ref[...] = grad_p[0:2, :]

    def part_e(d):
        g = lax.rem(x + d, 4)
        if d:
            copy(e_out.at[0], e_all.at[slice_of(g)], ss_e.at[0], rs_e.at[g], s, r).wait_recv()
        c_g = c_ref[:, lanes(g)]
        wide = pl.ds(pl.multiple_of(g * ROWS, ROWS), ROWS)

        def pair(j):
            i = g * PER + j
            entry = e_all[lanes(i), :]
            seen = mm_nt(c_g, entry)
            zz = cw[:, lanes(i)].astype(F32) * seen
            collect(i, zz, zz)
            prod = entry.astype(F32) * b_all[lanes(i), :].astype(F32)
            row = iota((8, LANE), 0)
            slot = 2 * lax.rem(i, 4)
            one = jnp.sum(jnp.where(top, prod, 0.0), axis=0, keepdims=True) * decay[pl.ds(2 * i, 1), :]
            two = jnp.sum(jnp.where(top, 0.0, prod), axis=0, keepdims=True) * decay[pl.ds(2 * i + 1, 1), :]
            at8 = pl.ds(pl.multiple_of(i // 4 * 8, 8), 8)
            add = jnp.where(row == slot, one, 0.0) + jnp.where(row == slot + 1, two, 0.0)
            car[at8, :] = car[at8, :] + add

        each(0, PER, pair)
        grad_c = mm(pooled[g].astype(BF16), b_ref[:, lanes(g)]) + mm(cw[:, wide], e_all[wide, :])
        gc_ref[:, lanes(g)] = grad_c.astype(BF16)

    keep = xs[...]
    for d in (0, 1, 3, 2):
        part_e(d)
    carried = jnp.sum(car[...], axis=1, keepdims=True)
    onward = (iota((TOK, TOK), 0) >= iota((TOK, TOK), 1)).astype(F32)
    grad_log = exact(zs[...], onward) + carried
    gdt_ref[...] = live * (keep / dt_ref[...] - rate_ref[...] * grad_log)

    wait_from(8, q, lambda k: copy(gb_all.at[k], gb_all.at[k], ss_gb.at[0], rs_gb.at[k], s, r))
    total = gb_all[0].astype(F32)
    for k in range(1, 8):
        total = total + gb_all[k].astype(F32)
    go_out[...] = total.astype(BF16)
    go_all[r] = total.astype(BF16)
    each(1, 32, lambda d: go_copy(d).start())
    wait_from(32, r, lambda k: copy(go_out, go_all.at[k], ss_go.at[0], rs_go.at[k], s, r))
    for k in range(32):
        gbp_ref[(k % 8) * 32 : (k % 8) * 32 + 32, (k // 8) * LANE : (k // 8 + 1) * LANE] = go_all[k]

    each(1, 8, lambda d: p_copy(d).wait_send())
    each(1, 8, lambda d: pd_copy(d).wait_send())
    for make in (d_copy, s_copy, l_copy, b_copy, e_copy):
        each(1, 4, lambda d: make(d).wait_send())
    z_copy().wait_send()
    each(1, 8, lambda d: gb_copy(d).wait_send())
    each(1, 32, lambda d: go_copy(d).wait_send())

    @pl.when((z == 0) & (y == x))
    def _():
        each(1, 32, lambda d: f_copy(d).wait_send())

    @pl.when(z == 0)
    def _():
        each(1, 32, lambda d: g_copy(d).wait_send())

        def q_sent(k):
            @pl.when(jnp.logical_not((k == s) & (y == x)))
            def _():
                q_copy(k).wait_send()

        each(0, 8, q_sent)


def local(
    x_prompt, dt_prompt, b_prompt, x_roll, dt_roll, b_roll, c_roll, rate, skip, grad_y, roll_len, prompt_len
):
    rate_b = jnp.broadcast_to(rate[:, None], (HEADS, LANE))
    skip_b = jnp.repeat(skip, 64)[None]
    vmem = pl.BlockSpec(memory_space=pltpu.VMEM)
    smem = pl.BlockSpec(memory_space=pltpu.SMEM)
    V = pltpu.VMEM
    dma = pltpu.SemaphoreType.DMA
    wide = HEADS * 64
    out = pl.pallas_call(
        kernel,
        name="mixer_backward",
        out_shape=(
            jax.ShapeDtypeStruct((PTOK, LANE), BF16),
            jax.ShapeDtypeStruct((PTOK, 512), BF16),
            jax.ShapeDtypeStruct((2, PTOK), F32),
            jax.ShapeDtypeStruct((TOK, wide), BF16),
            jax.ShapeDtypeStruct((TOK, 512), BF16),
            jax.ShapeDtypeStruct((TOK, 512), BF16),
            jax.ShapeDtypeStruct((HEADS, TOK), F32),
        ),
        in_specs=[vmem] * 10 + [smem] * 2,
        out_specs=(vmem,) * 7,
        scratch_shapes=[
            V((HEADS, TOK), F32), V((HEADS, TOK), F32), V((HEADS, TOK), F32), V((HEADS, LANE), F32),
            V((TOK, wide), BF16), V((TOK, wide), BF16), V((TOK, wide), BF16), V((TOK, wide), F32),
            V((GROUPS, TOK, TOK), F32), V((GROUPS, TOK, TOK), F32), V((TOK, wide), F32),
            V((HEADS, TOK), F32), V((HEADS, TOK), F32), V((HEADS, LANE), F32),
            V((wide, LANE), BF16), V((wide, LANE), BF16), V((4, ROWS, LANE), BF16), V((4, ROWS, LANE), BF16),
            V((4, 16, LANE), F32), V((ROWS, LANE), BF16), V((ROWS, LANE), BF16),
            V((4, ROWS, LANE), BF16), V((4, ROWS, LANE), BF16), V((wide, LANE), BF16), V((wide, LANE), BF16),
            V((8, LANE, LANE), BF16), V((8, LANE), F32), V((8, 8, LANE), F32), V((LANE, LANE), BF16),
            V((8, LANE, LANE), BF16), V((LANE, LANE), F32), V((PTOK, LANE), BF16), V((PTOK, LANE), F32),
            V((ROWS, LANE), BF16), V((32, 32, LANE), BF16), V((32, LANE), F32), V((4, 32, LANE), F32),
            V((PTOK, LANE), BF16), V((8, 32, LANE), BF16), V((32, LANE), BF16), V((32, 32, LANE), BF16),
            dma((8,)), dma((8,)), dma((8,)), dma((8,)), dma((4,)), dma((4,)), dma((4,)), dma((4,)),
            dma((4,)), dma((4,)), dma, dma,
            dma((32,)), dma((8,)), dma((4,)), dma((4,)), dma((4,)), dma((4,)), dma((32,)), dma((32,)),
            dma((8,)), dma((4,)), dma((8,)), dma((8,)), dma((32,)), dma((32,)),
        ],
        compiler_params=pltpu.CompilerParams(
            collective_id=0, has_side_effects=True, vmem_limit_bytes=48 * 1024 * 1024
        ),
        cost_estimate=pl.CostEstimate(flops=1_500_000_000, bytes_accessed=6_000_000, transcendentals=2_000_000),
    )(
        x_prompt, dt_prompt, b_prompt, x_roll[0], dt_roll[0], b_roll[0], c_roll[0], rate_b, skip_b, grad_y[0],
        roll_len, prompt_len,
    )
    gxp, gbp, gdtp, gx, gb, gc, gdt = out
    return gxp, gbp, gdtp, gx[None], gb[None], gc[None], gdt[None]


def solution(mesh):
    in_specs = (
        P("seq", "roll"), P("roll", "seq"), P("seq", None), P("roll", "seq", None), P("roll", None, "seq"),
        P("roll", "seq", None), P("roll", "seq", None), P(), P(), P("roll", "seq", None), P("roll"), P(),
    )
    out_specs = (
        P("seq", "roll"), P("seq", None), P("roll", "seq"), P("roll", "seq", None), P("roll", "seq", None),
        P("roll", "seq", None), P("roll", None, "seq"),
    )
    return jax.shard_map(local, mesh=mesh, in_specs=in_specs, out_specs=out_specs, check_vma=False)
```

```python
import functools

import jax
import jax.numpy as jnp
from jax import lax
from jax.experimental import pallas as pl
from jax.experimental.pallas import tpu as pltpu
from jax.sharding import PartitionSpec as P

MESH = pl.DeviceIdType.MESH
F32 = jnp.float32
BF16 = jnp.bfloat16
HEADS = 64
GROUPS = 4
TOK = 128
PTOK = 256
LANE = 128
PAIRS = 32
PER = 8
ROWS = 1024
EXACT = lax.Precision.HIGHEST


def iota(shape, axis):
    return lax.broadcasted_iota(jnp.int32, shape, axis)


def mm(a, b):
    return lax.dot_general(a, b, (((1,), (0,)), ((), ())), preferred_element_type=F32)


def mm_nt(a, b):
    return lax.dot_general(a, b, (((1,), (1,)), ((), ())), preferred_element_type=F32)


def mm_tn(a, b):
    return lax.dot_general(a, b, (((0,), (0,)), ((), ())), preferred_element_type=F32)


def exact(a, b):
    return lax.dot_general(a, b, (((1,), (0,)), ((), ())), preferred_element_type=F32, precision=EXACT)


def halves(value):
    high = value.astype(BF16)
    return high, (value - high.astype(F32)).astype(BF16)


def columns(first, second, rows, length):
    stacked = jnp.where(iota((rows, length), 0) < 64, first, second)
    return stacked.T


def each(first, last, act, unroll=1):
    def body(n, carry):
        for k in range(unroll):
            act(first + n * unroll + k)
        return carry

    lax.fori_loop(0, (last - first) // unroll, body, 0)


def kernel(
    xp_hbm, dtp_hbm, bp_hbm, x_hbm, dt_hbm, b_hbm, c_hbm, gy_hbm, rate_ref, skip_ref, len_ref, plen_ref,
    gxp_hbm, gbp_hbm, gdtp_hbm, gx_hbm, gb_hbm, gc_hbm, gdt_hbm,
    xp_ref, dtp_ref, bp_ref, x_ref, dt_ref, b_ref, c_ref, gy_ref,
    gxp_ref, gbp_ref, gdtp_ref, gx_ref, gb_ref, gc_ref, gdt_ref,
    rates, cum, wrow, step, decay, cot, xw, cw, wx, cb, pooled, dxi, zs, xs, car,
    s_loc, l_loc, s_all, l_all, dec_all, t_out, t_in, e_out, b_out, e_all, b_all,
    p_all, pdec, pdec_all, fork_all, enter_p, xw_p, wx_p,
    back, fg_all, fg_out, q_all, gbo, gb_all, go_all,
    in_sem, out_sem, ss_p, rs_p, ss_pd, rs_pd, ss_d, rs_d, ss_s, rs_s, ss_l, rs_l, ss_z, rs_z,
    ss_fy, ss_fr, rs_f, ss_b, rs_b, ss_e, rs_e, ss_g, rs_g, ss_q, rs_q, ss_gb, rs_gb, ss_gr, rs_gr, ss_gy, rs_gy,
):
    s = lax.axis_index("seq")
    r = lax.axis_index("roll")
    z, x = s // 4, s % 4
    y, q = r // 8, r % 8

    loads = [
        pltpu.make_async_copy(src, dst, in_sem.at[n])
        for n, (src, dst) in enumerate(
            (
                (dt_hbm, dt_ref), (gy_hbm, gy_ref), (c_hbm, c_ref), (dtp_hbm, dtp_ref), (xp_hbm, xp_ref),
                (bp_hbm, bp_ref), (x_hbm, x_ref), (b_hbm, b_ref),
            )
        )
    ]
    for load in loads:
        load.start()

    def at(seq, roll):
        return {"seq": seq, "roll": roll}

    def copy(src, dst, send, recv, seq, roll):
        return pltpu.make_async_remote_copy(
            src_ref=src, dst_ref=dst, send_sem=send, recv_sem=recv, device_id=at(seq, roll), device_id_type=MESH
        )

    bar = pltpu.get_barrier_semaphore()

    def greet(seq, roll):
        pl.semaphore_signal(bar, inc=1, device_id=at(seq, roll), device_id_type=MESH)

    def greet_quarter(k):
        @pl.when(jnp.logical_not((s == k // 4 * 4 + y) & (y == k % 4)))
        def _():
            greet(k // 4 * 4 + y, k % 4 * 8 + q)

    each(1, 8, lambda d: greet(lax.rem(s + d, 8), r))
    each(1, 32, lambda d: greet(s, lax.rem(r + d, 32)))
    each(0, 8, greet_quarter)

    for j in range(HEADS // 8):
        rows8 = jnp.full((8, LANE), rate_ref[8 * j], F32)
        for k in range(1, 8):
            rows8 = jnp.where(iota((8, LANE), 0) == k, rate_ref[8 * j + k], rows8)
        rates[8 * j : 8 * j + 8, :] = rows8
    live = (s * TOK + iota((1, TOK), 1) < len_ref[0]).astype(F32)
    loads[0].wait()
    step[...] = dt_ref[...] * live
    logd = -rates[...] * step[...]
    upto = (iota((TOK, TOK), 0) <= iota((TOK, TOK), 1)).astype(F32)
    cum_v = exact(logd, upto)
    end_v = exact(logd, jnp.ones((TOK, TOK), F32))
    cum[...] = cum_v
    decay[...] = jnp.exp(end_v)
    wrow[...] = step[...] * jnp.exp(end_v - cum_v)

    def slice_of(k):
        return pl.ds(pl.multiple_of(k * ROWS, ROWS), ROWS)

    def lanes(i):
        return pl.ds(pl.multiple_of(i * LANE, LANE), LANE)

    def p_copy(d):
        return copy(p_all.at[s], p_all.at[s], ss_p.at[d], rs_p.at[s], lax.rem(s + d, 8), r)

    def pd_copy(d):
        return copy(pdec, pdec_all.at[s], ss_pd.at[d], rs_pd.at[s], lax.rem(s + d, 8), r)

    def d_copy(d):
        to = lax.rem(s + d, 8)
        part = pl.ds(pl.multiple_of(to % 4 * 16, 16), 16)
        return copy(decay.at[part], dec_all.at[s], ss_d.at[d], rs_d.at[s], to, r)

    def s_copy(d):
        k = lax.rem(x + d, 4)
        return copy(s_loc.at[slice_of(k)], s_all.at[x], ss_s.at[d], rs_s.at[x], z * 4 + k, r)

    def l_copy(d):
        k = lax.rem(x + d, 4)
        return copy(l_loc.at[slice_of(k)], l_all.at[x], ss_l.at[d], rs_l.at[x], z * 4 + k, r)

    def z_copy():
        return copy(t_out, t_in, ss_z, rs_z, (1 - z) * 4 + x, r)

    def fy_copy(d):
        return copy(fork_all.at[q], fork_all.at[q], ss_fy.at[d], rs_f.at[q], s, lax.rem(r + 8 * d, 32))

    def fr_copy(d):
        return copy(fork_all.at[q], fork_all.at[q], ss_fr.at[d], rs_f.at[q], s, y * 8 + lax.rem(q + d, 8))

    def b_copy(d):
        k = lax.rem(x + d, 4)
        return copy(b_out.at[k], b_all.at[slice_of(x)], ss_b.at[d], rs_b.at[x], z * 4 + k, r)

    def e_copy(d):
        k = lax.rem(x + d, 4)
        return copy(e_out.at[k], e_all.at[slice_of(x)], ss_e.at[d], rs_e.at[x], z * 4 + k, r)

    def g_copy(d):
        t = lax.rem(r + d, 32)
        piece = pl.multiple_of(lax.rem(t, 8) * 128 + t // 8 * 32, 32)
        return copy(back.at[pl.ds(piece, 32)], fg_all.at[r], ss_g.at[d], rs_g.at[r], s, t)

    def q_copy(k):
        return copy(fg_out, q_all.at[z * 4 + y], ss_q.at[k], rs_q.at[z * 4 + y], k, x * 8 + q)

    def gb_copy(d):
        t = lax.rem(q + d, 8)
        return copy(gbo.at[pl.ds(pl.multiple_of(t * 32, 32), 32)], gb_all.at[q], ss_gb.at[d], rs_gb.at[q], s, y * 8 + t)

    def gr_copy(d):
        return copy(go_all.at[r], go_all.at[r], ss_gr.at[d], rs_gr.at[q], s, y * 8 + lax.rem(q + d, 8))

    def gy_copy(d):
        block = go_all.at[pl.ds(pl.multiple_of(y * 8, 8), 8)]
        return copy(block, block, ss_gy.at[d], rs_gy.at[y], s, lax.rem(r + 8 * d, 32))

    def wait_from(count, mine, make):
        each(1, count, lambda d: make(lax.rem(mine + d, count)).wait_recv())

    row_live = iota((TOK, LANE), 0) + s * TOK < len_ref[0]
    left = iota((TOK, LANE), 1) < 64
    top = iota((LANE, LANE), 0) < 64
    zero = jnp.zeros((LANE, LANE), F32)

    def s_pair(i, c_g):
        cx = columns(cum[pl.ds(2 * i, 1), :], cum[pl.ds(2 * i + 1, 1), :], LANE, TOK)
        ct = jnp.where(row_live, gy_ref[:, lanes(i)].astype(F32), 0.0)
        cot[:, lanes(i)] = ct.astype(BF16)
        weighted = (ct * jnp.exp(cx)).astype(BF16)
        cw[:, lanes(i)] = weighted
        s_loc[lanes(i), :] = mm_tn(weighted, c_g).astype(BF16)

    def l_pair(i, b_g):
        wide = columns(wrow[pl.ds(2 * i, 1), :], wrow[pl.ds(2 * i + 1, 1), :], LANE, TOK)
        wx[:, lanes(i)] = wide
        weighted = (x_ref[:, lanes(i)].astype(F32) * wide).astype(BF16)
        xw[:, lanes(i)] = weighted
        l_loc[lanes(i), :] = mm_tn(weighted, b_g).astype(BF16)

    loads[1].wait()
    loads[2].wait()
    for d in (2, 1, 3, 0):
        g = lax.rem(x + d, 4)
        c_g = c_ref[:, lanes(g)]
        each(0, PER, lambda i: s_pair(g * PER + i, c_g), 4)
        if d == 2:
            pl.semaphore_wait(bar, 46 - (y == x).astype(jnp.int32))
        if d:
            s_copy(d).start()
        else:
            s_all[x] = s_loc[slice_of(x), :]
    each(1, 8, lambda d: d_copy(d).start())
    dec_all[s] = decay[pl.ds(pl.multiple_of(x * 16, 16), 16), :]

    for n in (3, 4, 5):
        loads[n].wait()
    low8 = iota((8, PTOK), 0) < 1
    dtp = jnp.where(low8, dtp_ref[0:1, :], dtp_ref[1:2, :])
    ratep = jnp.where(low8, rate_ref[2 * r], rate_ref[2 * r + 1])
    first_live = 8 * PTOK - plen_ref[0]
    live_p = (s * PTOK + iota((1, PTOK), 1) >= first_live).astype(F32)
    step_p = dtp * live_p
    logd_p = -ratep * step_p
    upto_p = (iota((PTOK, PTOK), 0) <= iota((PTOK, PTOK), 1)).astype(F32)
    cum_p = exact(logd_p, upto_p)
    end_p = exact(logd_p, jnp.ones((PTOK, PTOK), F32))
    w_p = step_p * jnp.exp(end_p - cum_p)
    pdec[...] = jnp.exp(end_p[:, 0:LANE])
    wx_p[...] = columns(w_p[0:1, :], w_p[1:2, :], LANE, PTOK)
    xw_p[...] = (xp_ref[...].astype(F32) * wx_p[...]).astype(BF16)
    bp = bp_ref[:, lanes(y)]
    p_all[s] = mm_tn(xw_p[...], bp).astype(BF16)
    pdec_all[s] = pdec[...]
    each(1, 8, lambda d: p_copy(d).start())
    each(1, 8, lambda d: pd_copy(d).start())

    loads[6].wait()
    loads[7].wait()
    for g in range(GROUPS):
        b_g = b_ref[:, g * LANE : (g + 1) * LANE]
        each(0, PER, lambda i: l_pair(g * PER + i, b_g), 4)
    l_all[x] = l_loc[slice_of(x), :]

    for g in range(GROUPS):
        cb[g] = mm_nt(c_ref[:, g * LANE : (g + 1) * LANE], b_ref[:, g * LANE : (g + 1) * LANE])
        pooled[g] = zero
    zs[...] = jnp.zeros_like(zs)
    xs[...] = jnp.zeros_like(xs)
    car[...] = jnp.zeros_like(car)
    causal = iota((TOK, TOK), 0) >= iota((TOK, TOK), 1)

    def collect(i, zz, xd):
        z_hi, z_lo = halves(zz)
        row = iota((16, 3 * LANE), 0)
        lane = iota((16, 3 * LANE), 1)
        slot = 2 * lax.rem(i, 4) + (lax.rem(lane, LANE) >= 64).astype(jnp.int32)
        slot = slot + jnp.where(lane >= 2 * LANE, 8, 0)
        pick = (row == slot).astype(F32).astype(BF16)
        sums = mm_nt(pick, jnp.concatenate([z_hi, z_lo, xd.astype(BF16)], axis=1))
        at8 = pl.ds(pl.multiple_of(i // 4 * 8, 8), 8)
        zs[at8, :] = zs[at8, :] + sums[0:8]
        xs[at8, :] = xs[at8, :] + sums[8:16]

    def intra(i):
        g = i // PER
        xi = x_ref[:, lanes(i)]
        ci = cot[:, lanes(i)]
        xf = xi.astype(F32)
        cf = ci.astype(F32)
        both = jnp.concatenate([jnp.where(left, cf, 0.0).astype(BF16), jnp.where(left, 0.0, cf).astype(BF16)], axis=0)
        gx = mm_nt(both, xi)
        cbg = cb[g]
        mixes = []
        total = pooled[g]
        for a in range(2):
            row = cum[pl.ds(2 * i + a, 1), :]
            col = jnp.broadcast_to(row, (TOK, TOK)).T
            seg = jnp.where(causal, jnp.exp(col - row), 0.0) * step[pl.ds(2 * i + a, 1), :]
            total = total + seg * gx[a * TOK : (a + 1) * TOK]
            mixes.append((seg * cbg).astype(BF16))
        pooled[g] = total
        mix = jnp.concatenate(mixes, axis=0)
        dx = mm_tn(mix, both)
        yy = mm(mix, xi)
        yi = jnp.where(left, yy[:TOK], yy[TOK:])
        dxi[:, lanes(i)] = dx
        xd = xf * dx
        collect(i, cf * yi - xd, xd)

    each(0, 8, intra)

    wait_from(8, s, lambda k: copy(p_all.at[k], p_all.at[k], ss_p.at[0], rs_p.at[k], s, r))
    wait_from(8, s, lambda k: copy(pdec, pdec_all.at[k], ss_pd.at[0], rs_pd.at[k], s, r))
    enter_p[...] = zero
    fork = p_all[0].astype(F32)
    for k in range(1, 8):
        enter_p[...] = jnp.where(k == s, fork, enter_p[...])
        fork = jnp.where(top, pdec_all[k, 0:1, :], pdec_all[k, 1:2, :]) * fork + p_all[k].astype(F32)

    @pl.when((z == 0) & (y == x))
    def _():
        fork_all[q] = fork.astype(BF16)
        each(1, 4, lambda d: fy_copy(d).start())
        each(1, 8, lambda d: fr_copy(d).start())

    each(1, 4, lambda d: s_copy(d).wait_send())
    for d in (2, 1, 3):
        l_copy(d).start()
    each(8, 12, intra)

    def fork_slot(k):
        return copy(fork_all.at[k], fork_all.at[k], ss_fr.at[0], rs_f.at[k], s, r)

    @pl.when((z == 0) & (y != x))
    def _():
        fork_slot(q).wait_recv()
        each(1, 8, lambda d: fr_copy(d).start())

    wait_from(8, s, lambda k: copy(decay.at[pl.ds(0, 16)], dec_all.at[k], ss_d.at[0], rs_d.at[k], s, r))
    wait_from(4, x, lambda k: copy(s_all.at[k], s_all.at[k], ss_s.at[0], rs_s.at[k], s, r))

    def head_rows(h):
        return pl.ds(pl.multiple_of(h * 64, 64), 64)

    def give_back(out, whole, make):
        for d in (2, 1, 3):
            make(d).start()
        whole[slice_of(x), :] = out[x]

    def give_pieces():
        each(1, 32, lambda d: g_copy(d).start())
        fg_all[r] = back[pl.ds(pl.multiple_of(q * 128 + y * 32, 32), 32), :]

    @pl.when(z == 1)
    def _():
        def body(h):
            rows = head_rows(h)
            state = jnp.zeros((64, LANE), F32)
            for k in (3, 2, 1, 0):
                b_out[k, rows, :] = state.astype(BF16)
                state = dec_all[4 + k, pl.ds(h, 1), :] * state + s_all[k, rows, :].astype(F32)
            t_out[rows, :] = state.astype(BF16)
            for k in range(4):
                state = dec_all[k, pl.ds(h, 1), :] * state
            back[rows, :] = state.astype(BF16)

        each(0, 16, body)
        z_copy().start()
        give_pieces()
        give_back(b_out, b_all, b_copy)

    @pl.when(z == 0)
    def _():
        def body(h):
            rows = head_rows(h)
            state = s_all[3, rows, :].astype(F32)
            for k in (2, 1, 0):
                state = dec_all[k, pl.ds(h, 1), :] * state + s_all[k, rows, :].astype(F32)
            back[rows, :] = state.astype(BF16)

        each(0, 16, body)
        give_pieces()

    each(12, 24, intra)

    wait_from(32, r, lambda k: copy(fg_all.at[k], fg_all.at[k], ss_g.at[0], rs_g.at[k], s, r))
    total = fg_all[0].astype(F32)
    for k in range(1, 32):
        total = total + fg_all[k].astype(F32)
    fg_out[...] = total

    def q_send(k):
        @pl.when(jnp.logical_not((k == s) & (y == x)))
        def _():
            q_copy(k).start()

    each(0, 8, q_send)

    @pl.when(y == x)
    def _():
        q_all[z * 4 + y] = total

    each(24, 32, intra)

    @pl.when(z == 0)
    def _():
        z_copy().wait_recv()

        def body(h):
            rows = head_rows(h)
            state = t_in[rows, :].astype(F32)
            for k in (3, 2, 1, 0):
                b_out[k, rows, :] = state.astype(BF16)
                if k:
                    state = dec_all[k, pl.ds(h, 1), :] * state + s_all[k, rows, :].astype(F32)

        each(0, 16, body)
        give_back(b_out, b_all, b_copy)

    wait_from(4, x, lambda k: copy(l_all.at[k], l_all.at[k], ss_l.at[0], rs_l.at[k], s, r))

    @pl.when(z == 0)
    def _():
        wait_from(8, q, fork_slot)

        def body(h):
            rows = head_rows(h)
            state = fork_all[h // 2, pl.ds(pl.multiple_of(lax.rem(h, 2) * 64, 64), 64), :].astype(F32)
            for k in range(4):
                e_out[k, rows, :] = state.astype(BF16)
                state = dec_all[k, pl.ds(h, 1), :] * state + l_all[k, rows, :].astype(F32)
            t_out[rows, :] = state.astype(BF16)

        each(0, 16, body)
        z_copy().start()
        give_back(e_out, e_all, e_copy)

    def q_wait(k):
        @pl.when(jnp.logical_not((s == k // 4 * 4 + y) & (y == k % 4)))
        def _():
            copy(fg_out, q_all.at[k], ss_q.at[0], rs_q.at[k], s, r).wait_recv()

    each(0, 8, q_wait)
    q_whole = jnp.concatenate([q_all[k] + q_all[4 + k] for k in range(4)], axis=0)
    for k in range(1, 8):
        q_whole = q_whole * jnp.where(k > s, jnp.where(top, pdec_all[k, 0:1, :], pdec_all[k, 1:2, :]), 1.0)
    q_state = q_whole.astype(BF16)
    pulled_p = mm_nt(bp, q_state)
    dx_p = wx_p[...] * pulled_p
    gxp_ref[...] = dx_p.astype(BF16)
    gbo[...] = mm(xw_p[...], q_state)
    each(1, 8, lambda d: gb_copy(d).start())
    gb_all[q] = gbo[pl.ds(pl.multiple_of(q * 32, 32), 32), :]
    xd_p = xp_ref[...].astype(F32) * dx_p
    xd_hi, xd_lo = halves(xd_p)
    pick = (iota((8, 2 * LANE), 0) == (lax.rem(iota((8, 2 * LANE), 1), LANE) >= 64).astype(jnp.int32)).astype(F32)
    leave_p = mm_nt(pick.astype(BF16), jnp.concatenate([xd_hi, xd_lo], axis=1))
    before = (iota((PTOK, PTOK), 0) < iota((PTOK, PTOK), 1)).astype(F32)
    passed = exact(leave_p, before)
    meet = q_state.astype(F32) * enter_p[...]
    meet = jnp.where(
        iota((8, LANE), 0) < 1,
        jnp.sum(jnp.where(top, meet, 0.0), axis=0, keepdims=True),
        jnp.sum(jnp.where(top, 0.0, meet), axis=0, keepdims=True),
    )
    through = jnp.sum(meet * pdec[...], axis=1, keepdims=True)
    grad_p = live_p * (leave_p / dtp - ratep * (passed + through))
    gdtp_ref[...] = grad_p[0:2, :]

    def part_b(d):
        g = lax.rem(x + d, 4)
        if d:
            copy(b_out.at[0], b_all.at[slice_of(g)], ss_b.at[0], rs_b.at[g], s, r).wait_recv()
        b_g = b_ref[:, lanes(g)]
        wide = pl.ds(pl.multiple_of(g * ROWS, ROWS), ROWS)

        def pair(j):
            i = g * PER + j
            pulled = mm_nt(b_g, b_all[lanes(i), :])
            inter = wx[:, lanes(i)] * pulled
            xd = x_ref[:, lanes(i)].astype(F32) * inter
            gain = jnp.where(left, skip_ref[2 * i], skip_ref[2 * i + 1])
            grad = dxi[:, lanes(i)] + inter + gain * cot[:, lanes(i)].astype(F32)
            gx_ref[:, lanes(i)] = grad.astype(BF16)
            collect(i, -xd, xd)
            leave = jnp.sum(xd, axis=0, keepdims=True)
            row = iota((8, LANE), 0)
            slot = 2 * lax.rem(i, 4) + (iota((8, LANE), 1) >= 64).astype(jnp.int32)
            at8 = pl.ds(pl.multiple_of(i // 4 * 8, 8), 8)
            car[at8, :] = car[at8, :] + jnp.where(row == slot, leave, 0.0)

        each(0, PER, pair, 2)
        grad_b = mm_tn(pooled[g].astype(BF16), c_ref[:, lanes(g)]) + mm(xw[:, wide], b_all[wide, :])
        gb_ref[:, lanes(g)] = grad_b.astype(BF16)
        pltpu.make_async_copy(gx_ref.at[:, wide], gx_hbm.at[:, wide], out_sem.at[d]).start()

    def part_e(d):
        g = lax.rem(x + d, 4)
        if d:
            copy(e_out.at[0], e_all.at[slice_of(g)], ss_e.at[0], rs_e.at[g], s, r).wait_recv()
        c_g = c_ref[:, lanes(g)]
        wide = pl.ds(pl.multiple_of(g * ROWS, ROWS), ROWS)

        def pair(j):
            i = g * PER + j
            entry = e_all[lanes(i), :]
            seen = mm_nt(c_g, entry)
            z_hi, z_lo = halves(cw[:, lanes(i)].astype(F32) * seen)
            lane = iota((8, 2 * LANE), 1)
            slot = 2 * lax.rem(i, 4) + (lax.rem(lane, LANE) >= 64).astype(jnp.int32)
            pick = (iota((8, 2 * LANE), 0) == slot).astype(F32).astype(BF16)
            at8 = pl.ds(pl.multiple_of(i // 4 * 8, 8), 8)
            zs[at8, :] = zs[at8, :] + mm_nt(pick, jnp.concatenate([z_hi, z_lo], axis=1))
            prod = entry.astype(F32) * b_all[lanes(i), :].astype(F32)
            row = iota((8, LANE), 0)
            here = 2 * lax.rem(i, 4)
            one = jnp.sum(jnp.where(top, prod, 0.0), axis=0, keepdims=True) * decay[pl.ds(2 * i, 1), :]
            two = jnp.sum(jnp.where(top, 0.0, prod), axis=0, keepdims=True) * decay[pl.ds(2 * i + 1, 1), :]
            add = jnp.where(row == here, one, 0.0) + jnp.where(row == here + 1, two, 0.0)
            car[at8, :] = car[at8, :] + add

        each(0, PER, pair, 2)
        grad_c = mm(pooled[g].astype(BF16), b_ref[:, lanes(g)]) + mm(cw[:, wide], e_all[wide, :])
        gc_ref[:, lanes(g)] = grad_c.astype(BF16)

    part_b(0)
    part_b(1)

    @pl.when(z == 1)
    def _():
        z_copy().wait_recv()

        def body(h):
            rows = head_rows(h)
            state = t_in[rows, :].astype(F32)
            for k in range(4):
                e_out[k, rows, :] = state.astype(BF16)
                if k < 3:
                    state = dec_all[4 + k, pl.ds(h, 1), :] * state + l_all[k, rows, :].astype(F32)

        each(0, 16, body)
        give_back(e_out, e_all, e_copy)

    wait_from(8, q, lambda k: copy(gb_all.at[k], gb_all.at[k], ss_gb.at[0], rs_gb.at[k], s, r))
    total = gb_all[0]
    for k in range(1, 8):
        total = total + gb_all[k]
    go_all[r] = total.astype(BF16)
    each(1, 8, lambda d: gr_copy(d).start())

    part_b(3)
    part_b(2)
    wait_from(8, q, lambda k: copy(go_all.at[0], go_all.at[y * 8 + k], ss_gr.at[0], rs_gr.at[k], s, r))
    each(1, 4, lambda d: gy_copy(d).start())

    part_e(0)
    part_e(1)
    part_e(3)
    part_e(2)
    carried = jnp.sum(car[...], axis=1, keepdims=True)
    onward = (iota((TOK, TOK), 0) >= iota((TOK, TOK), 1)).astype(F32)
    grad_log = exact(zs[...], onward) + carried
    gdt_ref[...] = live * (xs[...] / dt_ref[...] - rates[...] * grad_log)

    def y_wait(k):
        block = go_all.at[pl.ds(pl.multiple_of(k * 8, 8), 8)]
        copy(block, block, ss_gy.at[0], rs_gy.at[k], s, r).wait_recv()

    each(1, 4, lambda d: y_wait(lax.rem(y + d, 4)))
    for k in range(32):
        gbp_ref[(k % 8) * 32 : (k % 8) * 32 + 32, (k // 8) * LANE : (k // 8 + 1) * LANE] = go_all[k]
    stores = [
        pltpu.make_async_copy(src, dst, out_sem.at[4 + n])
        for n, (src, dst) in enumerate(
            (
                (gxp_ref, gxp_hbm), (gbp_ref, gbp_hbm), (gdtp_ref, gdtp_hbm), (gb_ref, gb_hbm), (gc_ref, gc_hbm),
                (gdt_ref, gdt_hbm),
            )
        )
    ]
    for store in stores:
        store.start()

    each(1, 8, lambda d: p_copy(d).wait_send())
    each(1, 8, lambda d: pd_copy(d).wait_send())
    each(1, 8, lambda d: d_copy(d).wait_send())
    for make in (l_copy, b_copy, e_copy):
        each(1, 4, lambda d: make(d).wait_send())
    z_copy().wait_send()
    each(1, 8, lambda d: gb_copy(d).wait_send())
    each(1, 8, lambda d: gr_copy(d).wait_send())
    each(1, 4, lambda d: gy_copy(d).wait_send())
    each(1, 32, lambda d: g_copy(d).wait_send())

    @pl.when(z == 0)
    def _():
        each(1, 8, lambda d: fr_copy(d).wait_send())

    @pl.when((z == 0) & (y == x))
    def _():
        each(1, 4, lambda d: fy_copy(d).wait_send())

    def q_sent(k):
        @pl.when(jnp.logical_not((k == s) & (y == x)))
        def _():
            q_copy(k).wait_send()

    each(0, 8, q_sent)
    for d in range(4):
        wide = pl.ds(pl.multiple_of(lax.rem(x + d, 4) * ROWS, ROWS), ROWS)
        pltpu.make_async_copy(gx_ref.at[:, wide], gx_hbm.at[:, wide], out_sem.at[d]).wait()
    for store in stores:
        store.wait()


def hand_on(*refs):
    count = (len(refs) - 1) // 2
    moves = [pltpu.make_async_copy(refs[n], refs[count + n], refs[-1].at[n]) for n in range(count)]
    for move in moves:
        move.start()
    for move in moves:
        move.wait()


def local(
    x_prompt, dt_prompt, b_prompt, x_roll, dt_roll, b_roll, c_roll, rate, skip, grad_y, roll_len, prompt_len
):
    anywhere = pl.BlockSpec(memory_space=pl.ANY)
    smem = pl.BlockSpec(memory_space=pltpu.SMEM)
    V = pltpu.VMEM
    dma = pltpu.SemaphoreType.DMA
    wide = HEADS * 64
    ins = (x_prompt, dt_prompt, b_prompt, x_roll[0], dt_roll[0], b_roll[0], c_roll[0], grad_y[0])
    outs = (
        jax.ShapeDtypeStruct((PTOK, LANE), BF16),
        jax.ShapeDtypeStruct((PTOK, 512), BF16),
        jax.ShapeDtypeStruct((2, PTOK), F32),
        jax.ShapeDtypeStruct((TOK, wide), BF16),
        jax.ShapeDtypeStruct((TOK, 512), BF16),
        jax.ShapeDtypeStruct((TOK, 512), BF16),
        jax.ShapeDtypeStruct((HEADS, TOK), F32),
    )
    out = pl.pallas_call(
        kernel,
        name="mixer_backward",
        out_shape=outs,
        in_specs=[anywhere] * 8 + [smem] * 4,
        out_specs=(anywhere,) * 7,
        scratch_shapes=[V(value.shape, value.dtype) for value in ins + outs]
        + [
            V((HEADS, LANE), F32), V((HEADS, TOK), F32), V((HEADS, TOK), F32), V((HEADS, TOK), F32), V((HEADS, LANE), F32),
            V((TOK, wide), BF16), V((TOK, wide), BF16), V((TOK, wide), BF16), V((TOK, wide), F32),
            V((GROUPS, TOK, TOK), F32), V((GROUPS, TOK, TOK), F32), V((TOK, wide), F32),
            V((HEADS, TOK), F32), V((HEADS, TOK), F32), V((HEADS, LANE), F32),
            V((wide, LANE), BF16), V((wide, LANE), BF16), V((4, ROWS, LANE), BF16), V((4, ROWS, LANE), BF16),
            V((8, 16, LANE), F32), V((ROWS, LANE), BF16), V((ROWS, LANE), BF16),
            V((4, ROWS, LANE), BF16), V((4, ROWS, LANE), BF16), V((wide, LANE), BF16), V((wide, LANE), BF16),
            V((8, LANE, LANE), BF16), V((8, LANE), F32), V((8, 8, LANE), F32),
            V((8, LANE, LANE), BF16), V((LANE, LANE), F32), V((PTOK, LANE), BF16), V((PTOK, LANE), F32),
            V((ROWS, LANE), BF16), V((32, 32, LANE), BF16), V((32, LANE), F32), V((8, 32, LANE), F32),
            V((PTOK, LANE), F32), V((8, 32, LANE), F32), V((32, 32, LANE), BF16),
            dma((8,)), dma((10,)), dma((8,)), dma((8,)), dma((8,)), dma((8,)), dma((8,)), dma((8,)),
            dma((4,)), dma((4,)), dma((4,)), dma((4,)), dma, dma,
            dma((4,)), dma((8,)), dma((8,)), dma((4,)), dma((4,)), dma((4,)), dma((4,)), dma((32,)), dma((32,)),
            dma((8,)), dma((8,)), dma((8,)), dma((8,)), dma((8,)), dma((8,)), dma((4,)), dma((4,)),
        ],
        compiler_params=pltpu.CompilerParams(
            collective_id=0, has_side_effects=True, vmem_limit_bytes=60 * 1024 * 1024
        ),
        cost_estimate=pl.CostEstimate(flops=1_500_000_000, bytes_accessed=6_000_000, transcendentals=2_000_000),
    )(*ins, rate, skip, roll_len, prompt_len)
    out = pl.pallas_call(
        hand_on,
        name="hand_on",
        out_shape=outs,
        in_specs=[pl.BlockSpec(memory_space=pltpu.VMEM)] * 7,
        out_specs=(anywhere,) * 7,
        scratch_shapes=[dma((7,))],
    )(*out)
    gxp, gbp, gdtp, gx, gb, gc, gdt = out
    return gxp, gbp, gdtp, gx[None], gb[None], gc[None], gdt[None]


def solution(mesh):
    in_specs = (
        P("seq", "roll"), P("roll", "seq"), P("seq", None), P("roll", "seq", None), P("roll", None, "seq"),
        P("roll", "seq", None), P("roll", "seq", None), P(), P(), P("roll", "seq", None), P("roll"), P(),
    )
    out_specs = (
        P("seq", "roll"), P("seq", None), P("roll", "seq"), P("roll", "seq", None), P("roll", "seq", None),
        P("roll", "seq", None), P("roll", None, "seq"),
    )
    return jax.shard_map(local, mesh=mesh, in_specs=in_specs, out_specs=out_specs, check_vma=False)
```

```python
import functools

import jax
import jax.numpy as jnp
from jax import lax
from jax.experimental import pallas as pl
from jax.experimental.pallas import tpu as pltpu
from jax.sharding import PartitionSpec as P

MESH = pl.DeviceIdType.MESH
F32 = jnp.float32
BF16 = jnp.bfloat16
HEADS = 64
GROUPS = 4
TOK = 128
PTOK = 256
LANE = 128
PAIRS = 32
PER = 8
ROWS = 1024
EXACT = lax.Precision.HIGHEST


def iota(shape, axis):
    return lax.broadcasted_iota(jnp.int32, shape, axis)


def mm(a, b):
    return lax.dot_general(a, b, (((1,), (0,)), ((), ())), preferred_element_type=F32)


def mm_nt(a, b):
    return lax.dot_general(a, b, (((1,), (1,)), ((), ())), preferred_element_type=F32)


def mm_tn(a, b):
    return lax.dot_general(a, b, (((0,), (0,)), ((), ())), preferred_element_type=F32)


def exact(a, b):
    return lax.dot_general(a, b, (((1,), (0,)), ((), ())), preferred_element_type=F32, precision=EXACT)


def halves(value):
    high = value.astype(BF16)
    return high, (value - high.astype(F32)).astype(BF16)


def columns(first, second, rows, length):
    stacked = jnp.where(iota((rows, length), 0) < 64, first, second)
    return stacked.T


def each(first, last, act, unroll=1):
    def body(n, carry):
        for k in range(unroll):
            act(first + n * unroll + k)
        return carry

    lax.fori_loop(0, (last - first) // unroll, body, 0)


def kernel(
    xp_hbm, dtp_hbm, bp_hbm, x_hbm, dt_hbm, b_hbm, c_hbm, gy_hbm, rate_ref, skip_ref, len_ref, plen_ref,
    gxp_hbm, gbp_hbm, gdtp_hbm, gx_hbm, gb_hbm, gc_hbm, gdt_hbm,
    xp_ref, dtp_ref, bp_ref, x_ref, dt_ref, b_ref, c_ref, gy_ref,
    gxp_ref, gbp_ref, gdtp_ref, gx_ref, gb_ref, gc_ref, gdt_ref,
    rates, cum, wrow, step, decay, cot, xw, cw, wx, cb, pooled, dxi, zs, xs, car,
    s_loc, l_loc, s_all, l_all, dec_all, t_out, t_in, e_out, b_out, e_all, b_all,
    p_all, pdec, pdec_all, half_out, half_in, hdec_out, hdec_in, fork_all, enter_p, xw_p, wx_p,
    back, sib_in, fg_pieces, fg_all, fg_out, q_all, gbo, gb_all, go_all,
    in_sem, out_sem, ss_p, rs_p, ss_pd, rs_pd, ss_d, rs_d, ss_s, rs_s, ss_l, rs_l, ss_z, rs_z,
    ss_h, rs_h, ss_fy, ss_fr, rs_f, ss_fc, rs_fc, ss_k, rs_k, ss_b, rs_b, ss_e, rs_e, ss_g, rs_g, ss_q, rs_q, ss_gb, rs_gb, ss_gr, rs_gr, ss_gy, rs_gy,
):
    s = lax.axis_index("seq")
    r = lax.axis_index("roll")
    z, x = s // 4, s % 4
    y, q = r // 8, r % 8
    deep, core = q // 2, q % 2
    sibling = r + 1 - 2 * core

    loads = [
        pltpu.make_async_copy(src, dst, in_sem.at[n])
        for n, (src, dst) in enumerate(
            (
                (dt_hbm, dt_ref), (gy_hbm, gy_ref), (c_hbm, c_ref), (dtp_hbm, dtp_ref), (xp_hbm, xp_ref),
                (bp_hbm, bp_ref), (x_hbm, x_ref), (b_hbm, b_ref),
            )
        )
    ]
    for load in loads:
        load.start()

    def at(seq, roll):
        return {"seq": seq, "roll": roll}

    def copy(src, dst, send, recv, seq, roll):
        return pltpu.make_async_remote_copy(
            src_ref=src, dst_ref=dst, send_sem=send, recv_sem=recv, device_id=at(seq, roll), device_id_type=MESH
        )

    bar = pltpu.get_barrier_semaphore()

    def greet(seq, roll):
        pl.semaphore_signal(bar, inc=1, device_id=at(seq, roll), device_id_type=MESH)

    def greet_quarter(k):
        @pl.when(jnp.logical_not((s == k // 4 * 4 + y) & (y == k % 4)))
        def _():
            greet(k // 4 * 4 + y, k % 4 * 8 + q)

    each(1, 8, lambda d: greet(lax.rem(s + d, 8), r))
    each(1, 32, lambda d: greet(s, lax.rem(r + d, 32)))
    each(0, 8, greet_quarter)

    for j in range(HEADS // 8):
        rows8 = jnp.full((8, LANE), rate_ref[8 * j], F32)
        for k in range(1, 8):
            rows8 = jnp.where(iota((8, LANE), 0) == k, rate_ref[8 * j + k], rows8)
        rates[8 * j : 8 * j + 8, :] = rows8
    live = (s * TOK + iota((1, TOK), 1) < len_ref[0]).astype(F32)
    loads[0].wait()
    step[...] = dt_ref[...] * live
    logd = -rates[...] * step[...]
    upto = (iota((TOK, TOK), 0) <= iota((TOK, TOK), 1)).astype(F32)
    cum_v = exact(logd, upto)
    end_v = exact(logd, jnp.ones((TOK, TOK), F32))
    cum[...] = cum_v
    decay[...] = jnp.exp(end_v)
    wrow[...] = step[...] * jnp.exp(end_v - cum_v)

    def slice_of(k):
        return pl.ds(pl.multiple_of(k * ROWS, ROWS), ROWS)

    def lanes(i):
        return pl.ds(pl.multiple_of(i * LANE, LANE), LANE)

    def p_copy(d):
        return copy(p_all.at[x], p_all.at[x], ss_p.at[d], rs_p.at[x], z * 4 + lax.rem(x + d, 4), r)

    def pd_copy(d):
        return copy(pdec, pdec_all.at[x], ss_pd.at[d], rs_pd.at[x], z * 4 + lax.rem(x + d, 4), r)

    def h_copy(n):
        out, there = ((half_out, half_in), (hdec_out, hdec_in))[n]
        return copy(out, there, ss_h.at[n], rs_h.at[n], (1 - z) * 4 + x, r)

    def d_copy(d):
        to = lax.rem(s + d, 8)
        part = pl.ds(pl.multiple_of(to % 4 * 16, 16), 16)
        return copy(decay.at[part], dec_all.at[s], ss_d.at[d], rs_d.at[s], to, r)

    def s_copy(d):
        k = lax.rem(x + d, 4)
        return copy(s_loc.at[slice_of(k)], s_all.at[x], ss_s.at[d], rs_s.at[x], z * 4 + k, r)

    def l_copy(d):
        k = lax.rem(x + d, 4)
        return copy(l_loc.at[slice_of(k)], l_all.at[x], ss_l.at[d], rs_l.at[x], z * 4 + k, r)

    def z_copy(n):
        part = pl.ds(n * (ROWS // 2), ROWS // 2)
        return copy(t_out.at[part], t_in.at[part], ss_z.at[n], rs_z.at[n], (1 - z) * 4 + x, r)

    def fy_copy(d):
        mine = fork_all.at[core, deep]
        return copy(mine, mine, ss_fy.at[d], rs_f.at[deep], s, lax.rem(r + 8 * d, 32))

    def fr_copy(d):
        mine = fork_all.at[core, deep]
        return copy(mine, mine, ss_fr.at[d], rs_f.at[deep], s, y * 8 + lax.rem(deep + d, 4) * 2 + core)

    def fc_copy():
        return copy(fork_all.at[core], fork_all.at[core], ss_fc, rs_fc, s, sibling)

    def part_of(k, n):
        return pl.ds(pl.multiple_of(k * ROWS + n * (ROWS // 2), ROWS // 2), ROWS // 2)

    def b_copy(d, n):
        k = lax.rem(x + d, 4)
        src = b_out.at[k, pl.ds(n * (ROWS // 2), ROWS // 2)]
        return copy(src, b_all.at[part_of(x, n)], ss_b.at[2 * d + n], rs_b.at[2 * x + n], z * 4 + k, r)

    def e_copy(d, n):
        k = lax.rem(x + d, 4)
        src = e_out.at[k, pl.ds(n * (ROWS // 2), ROWS // 2)]
        return copy(src, e_all.at[part_of(x, n)], ss_e.at[2 * d + n], rs_e.at[2 * x + n], z * 4 + k, r)

    def k_copy():
        return copy(back.at[1 - core], sib_in, ss_k, rs_k, s, sibling)

    mine = y * 4 + deep

    def g_copy(d):
        t = lax.rem(mine + d, 16)
        piece = pl.ds(pl.multiple_of(lax.rem(t, 4) * 128 + t // 4 * 32, 32), 32)
        return copy(
            fg_pieces.at[piece], fg_all.at[mine], ss_g.at[d], rs_g.at[mine], s, t // 4 * 8 + lax.rem(t, 4) * 2 + core
        )

    def q_copy(k):
        return copy(fg_out, q_all.at[z * 4 + y], ss_q.at[k], rs_q.at[z * 4 + y], k, x * 8 + q)

    def gb_copy(d):
        t = lax.rem(q + d, 8)
        return copy(gbo.at[pl.ds(pl.multiple_of(t * 32, 32), 32)], gb_all.at[q], ss_gb.at[d], rs_gb.at[q], s, y * 8 + t)

    def gr_copy(d):
        return copy(go_all.at[r], go_all.at[r], ss_gr.at[d], rs_gr.at[q], s, y * 8 + lax.rem(q + d, 8))

    def gy_copy(d):
        block = go_all.at[pl.ds(pl.multiple_of(y * 8, 8), 8)]
        return copy(block, block, ss_gy.at[d], rs_gy.at[y], s, lax.rem(r + 8 * d, 32))

    def wait_from(count, mine, make):
        each(1, count, lambda d: make(lax.rem(mine + d, count)).wait_recv())

    row_live = iota((TOK, LANE), 0) + s * TOK < len_ref[0]
    left = iota((TOK, LANE), 1) < 64
    top = iota((LANE, LANE), 0) < 64
    zero = jnp.zeros((LANE, LANE), F32)

    def s_pair(i, c_g):
        cx = columns(cum[pl.ds(2 * i, 1), :], cum[pl.ds(2 * i + 1, 1), :], LANE, TOK)
        ct = jnp.where(row_live, gy_ref[:, lanes(i)].astype(F32), 0.0)
        cot[:, lanes(i)] = ct.astype(BF16)
        weighted = (ct * jnp.exp(cx)).astype(BF16)
        cw[:, lanes(i)] = weighted
        s_loc[lanes(i), :] = mm_tn(weighted, c_g).astype(BF16)

    def l_pair(i, b_g):
        wide = columns(wrow[pl.ds(2 * i, 1), :], wrow[pl.ds(2 * i + 1, 1), :], LANE, TOK)
        wx[:, lanes(i)] = wide
        weighted = (x_ref[:, lanes(i)].astype(F32) * wide).astype(BF16)
        xw[:, lanes(i)] = weighted
        l_loc[lanes(i), :] = mm_tn(weighted, b_g).astype(BF16)

    loads[1].wait()
    loads[2].wait()
    def summarize(d):
        g = lax.rem(x + d, 4)
        c_g = c_ref[:, lanes(g)]
        each(0, PER, lambda i: s_pair(g * PER + i, c_g), 4)

    summarize(2)
    pl.semaphore_wait(bar, 46 - (y == x).astype(jnp.int32))
    s_copy(2).start()
    each(1, 8, lambda d: d_copy(d).start())
    dec_all[s] = decay[pl.ds(pl.multiple_of(x * 16, 16), 16), :]

    for n in (3, 4, 5):
        loads[n].wait()
    low8 = iota((8, PTOK), 0) < 1
    dtp = jnp.where(low8, dtp_ref[0:1, :], dtp_ref[1:2, :])
    ratep = jnp.where(low8, rate_ref[2 * r], rate_ref[2 * r + 1])
    first_live = 8 * PTOK - plen_ref[0]
    live_p = (s * PTOK + iota((1, PTOK), 1) >= first_live).astype(F32)
    step_p = dtp * live_p
    logd_p = -ratep * step_p
    upto_p = (iota((PTOK, PTOK), 0) <= iota((PTOK, PTOK), 1)).astype(F32)
    cum_p = exact(logd_p, upto_p)
    end_p = exact(logd_p, jnp.ones((PTOK, PTOK), F32))
    w_p = step_p * jnp.exp(end_p - cum_p)
    pdec[...] = jnp.exp(end_p[:, 0:LANE])
    wx_p[...] = columns(w_p[0:1, :], w_p[1:2, :], LANE, PTOK)
    xw_p[...] = (xp_ref[...].astype(F32) * wx_p[...]).astype(BF16)
    bp = bp_ref[:, lanes(y)]
    p_all[x] = mm_tn(xw_p[...], bp).astype(BF16)
    pdec_all[x] = pdec[...]
    each(1, 4, lambda d: p_copy(d).start())
    each(1, 4, lambda d: pd_copy(d).start())

    for d in (1, 3):
        summarize(d)
        s_copy(d).start()
    summarize(0)
    s_all[x] = s_loc[slice_of(x), :]

    loads[6].wait()
    loads[7].wait()
    for g in range(GROUPS):
        b_g = b_ref[:, g * LANE : (g + 1) * LANE]
        each(0, PER, lambda i: l_pair(g * PER + i, b_g), 4)
    l_all[x] = l_loc[slice_of(x), :]

    wait_from(4, x, lambda k: copy(p_all.at[k], p_all.at[k], ss_p.at[0], rs_p.at[k], s, r))
    wait_from(4, x, lambda k: copy(pdec, pdec_all.at[k], ss_pd.at[0], rs_pd.at[k], s, r))

    def pdecay(ref):
        return jnp.where(top, ref[0:1, :], ref[1:2, :])

    half = p_all[0].astype(F32)
    hdec = pdec_all[0]
    for k in range(1, 4):
        half = pdecay(pdec_all.at[k]) * half + p_all[k].astype(F32)
        hdec = hdec * pdec_all[k]
    half_out[...] = half.astype(BF16)
    hdec_out[...] = hdec
    h_copy(0).start()
    h_copy(1).start()

    for g in range(GROUPS):
        cb[g] = mm_nt(c_ref[:, g * LANE : (g + 1) * LANE], b_ref[:, g * LANE : (g + 1) * LANE])
        pooled[g] = zero
    zs[...] = jnp.zeros_like(zs)
    xs[...] = jnp.zeros_like(xs)
    car[...] = jnp.zeros_like(car)
    causal = iota((TOK, TOK), 0) >= iota((TOK, TOK), 1)

    def collect(i, zz, xd):
        z_hi, z_lo = halves(zz)
        row = iota((16, 3 * LANE), 0)
        lane = iota((16, 3 * LANE), 1)
        slot = 2 * lax.rem(i, 4) + (lax.rem(lane, LANE) >= 64).astype(jnp.int32)
        slot = slot + jnp.where(lane >= 2 * LANE, 8, 0)
        pick = (row == slot).astype(F32).astype(BF16)
        sums = mm_nt(pick, jnp.concatenate([z_hi, z_lo, xd.astype(BF16)], axis=1))
        at8 = pl.ds(pl.multiple_of(i // 4 * 8, 8), 8)
        zs[at8, :] = zs[at8, :] + sums[0:8]
        xs[at8, :] = xs[at8, :] + sums[8:16]

    def intra(i):
        g = i // PER
        xi = x_ref[:, lanes(i)]
        ci = cot[:, lanes(i)]
        xf = xi.astype(F32)
        cf = ci.astype(F32)
        both = jnp.concatenate([jnp.where(left, cf, 0.0).astype(BF16), jnp.where(left, 0.0, cf).astype(BF16)], axis=0)
        gx = mm_nt(both, xi)
        cbg = cb[g]
        mixes = []
        total = pooled[g]
        for a in range(2):
            row = cum[pl.ds(2 * i + a, 1), :]
            col = jnp.broadcast_to(row, (TOK, TOK)).T
            seg = jnp.where(causal, jnp.exp(col - row), 0.0) * step[pl.ds(2 * i + a, 1), :]
            total = total + seg * gx[a * TOK : (a + 1) * TOK]
            mixes.append((seg * cbg).astype(BF16))
        pooled[g] = total
        mix = jnp.concatenate(mixes, axis=0)
        dx = mm_tn(mix, both)
        yy = mm(mix, xi)
        yi = jnp.where(left, yy[:TOK], yy[TOK:])
        dxi[:, lanes(i)] = dx
        xd = xf * dx
        collect(i, cf * yi - xd, xd)

    each(0, 6, intra)

    each(1, 4, lambda d: s_copy(d).wait_send())
    for d in (2, 1, 3):
        l_copy(d).start()

    h_copy(0).wait_recv()
    h_copy(1).wait_recv()
    enter_p[...] = jnp.where(z == 1, half_in[...].astype(F32), 0.0)
    for k in range(3):
        moved = pdecay(pdec_all.at[k]) * enter_p[...] + p_all[k].astype(F32)
        enter_p[...] = jnp.where(k < x, moved, enter_p[...])

    @pl.when((z == 0) & (y == x))
    def _():
        fork_all[core, deep] = (pdecay(hdec_in) * half + half_in[...].astype(F32)).astype(BF16)
        each(1, 4, lambda d: fy_copy(d).start())
        each(1, 4, lambda d: fr_copy(d).start())

    def fork_slot(k):
        slot = fork_all.at[core, k]
        return copy(slot, slot, ss_fr.at[0], rs_f.at[k], s, r)

    wait_from(8, s, lambda k: copy(decay.at[pl.ds(0, 16)], dec_all.at[k], ss_d.at[0], rs_d.at[k], s, r))
    wait_from(4, x, lambda k: copy(s_all.at[k], s_all.at[k], ss_s.at[0], rs_s.at[k], s, r))

    def head_rows(h):
        return pl.ds(pl.multiple_of(h * 64, 64), 64)

    def give_back(out, whole, make, n):
        for d in (2, 1, 3):
            make(d, n).start()
        whole[part_of(x, n), :] = out[x, n * (ROWS // 2) : (n + 1) * (ROWS // 2), :]

    def keep_back(h, state):
        rows = pl.ds(pl.multiple_of(h // 4 * 128 + lax.rem(h, 2) * 64, 64), 64)
        back[lax.rem(h // 2, 2), rows, :] = state.astype(BF16)

    @pl.when(z == 1)
    def _():
        def body(h):
            rows = head_rows(h)
            state = jnp.zeros((64, LANE), F32)
            for k in (3, 2, 1, 0):
                b_out[k, rows, :] = state.astype(BF16)
                state = dec_all[4 + k, pl.ds(h, 1), :] * state + s_all[k, rows, :].astype(F32)
            t_out[rows, :] = state.astype(BF16)
            for k in range(4):
                state = dec_all[k, pl.ds(h, 1), :] * state
            keep_back(h, state)

        for n in range(2):
            each(8 * n, 8 * n + 8, body, 2)
            z_copy(n).start()
        k_copy().start()

    @pl.when(z == 0)
    def _():
        def body(h):
            rows = head_rows(h)
            state = s_all[3, rows, :].astype(F32)
            for k in (2, 1, 0):
                state = dec_all[k, pl.ds(h, 1), :] * state + s_all[k, rows, :].astype(F32)
            keep_back(h, state)

        each(0, 16, body, 2)
        k_copy().start()

    @pl.when((z == 0) & (y != x))
    def _():
        fork_slot(deep).wait_recv()
        each(1, 4, lambda d: fr_copy(d).start())

    each(6, 8, intra)

    k_copy().wait_recv()
    fg_pieces[...] = (back[core].astype(F32) + sib_in[...].astype(F32)).astype(BF16)
    each(1, 16, lambda d: g_copy(d).start())
    fg_all[mine] = fg_pieces[pl.ds(pl.multiple_of(deep * 128 + y * 32, 32), 32), :]

    @pl.when(z == 0)
    def _():
        wait_from(4, deep, fork_slot)
        fc_copy().start()

    each(8, 14, intra)

    wait_from(16, mine, lambda k: copy(fg_all.at[k], fg_all.at[k], ss_g.at[0], rs_g.at[k], s, r))
    total = fg_all[0].astype(F32)
    for k in range(1, 16):
        total = total + fg_all[k].astype(F32)
    fg_out[...] = total

    def q_send(k):
        @pl.when(jnp.logical_not((k == s) & (y == x)))
        def _():
            q_copy(k).start()

    each(0, 8, q_send)

    @pl.when(y == x)
    def _():
        q_all[z * 4 + y] = total

    def leave(h):
        rows = head_rows(h)
        state = t_in[rows, :].astype(F32)
        for k in (3, 2, 1, 0):
            b_out[k, rows, :] = state.astype(BF16)
            if k:
                state = dec_all[k, pl.ds(h, 1), :] * state + s_all[k, rows, :].astype(F32)

    def leave_half(n):
        z_copy(n).wait_recv()
        each(8 * n, 8 * n + 8, leave, 2)
        give_back(b_out, b_all, b_copy, n)

    @pl.when(z == 1)
    def _():
        for n in range(2):
            give_back(b_out, b_all, b_copy, n)

    @pl.when(z == 0)
    def _():
        leave_half(0)

    @pl.when(z == 0)
    def _():
        wait_from(4, x, lambda k: copy(l_all.at[k], l_all.at[k], ss_l.at[0], rs_l.at[k], s, r))
        copy(fork_all.at[0], fork_all.at[1 - core], ss_fc, rs_fc, s, r).wait_recv()

        def enter(h):
            rows = head_rows(h)
            first = pl.ds(pl.multiple_of(lax.rem(h, 2) * 64, 64), 64)
            state = fork_all[lax.rem(h // 2, 2), h // 4, first, :].astype(F32)
            for k in range(4):
                e_out[k, rows, :] = state.astype(BF16)
                state = dec_all[k, pl.ds(h, 1), :] * state + l_all[k, rows, :].astype(F32)
            t_out[rows, :] = state.astype(BF16)

        for n in range(2):
            each(8 * n, 8 * n + 8, enter, 2)
            z_copy(n).start()
        leave_half(1)
        for n in range(2):
            give_back(e_out, e_all, e_copy, n)

    each(14, 24, intra)

    def q_wait(k):
        @pl.when(jnp.logical_not((s == k // 4 * 4 + y) & (y == k % 4)))
        def _():
            copy(fg_out, q_all.at[k], ss_q.at[0], rs_q.at[k], s, r).wait_recv()

    each(0, 8, q_wait)
    q_whole = jnp.concatenate([q_all[k] + q_all[4 + k] for k in range(4)], axis=0)
    q_whole = q_whole * jnp.where(z == 0, pdecay(hdec_in), 1.0)
    for k in range(1, 4):
        q_whole = q_whole * jnp.where(k > x, pdecay(pdec_all.at[k]), 1.0)
    q_state = q_whole.astype(BF16)
    pulled_p = mm_nt(bp, q_state)
    dx_p = wx_p[...] * pulled_p
    gxp_ref[...] = dx_p.astype(BF16)
    gbo[...] = mm(xw_p[...], q_state)
    each(1, 8, lambda d: gb_copy(d).start())
    gb_all[q] = gbo[pl.ds(pl.multiple_of(q * 32, 32), 32), :]
    xd_p = xp_ref[...].astype(F32) * dx_p
    xd_hi, xd_lo = halves(xd_p)
    pick = (iota((8, 2 * LANE), 0) == (lax.rem(iota((8, 2 * LANE), 1), LANE) >= 64).astype(jnp.int32)).astype(F32)
    leave_p = mm_nt(pick.astype(BF16), jnp.concatenate([xd_hi, xd_lo], axis=1))
    before = (iota((PTOK, PTOK), 0) < iota((PTOK, PTOK), 1)).astype(F32)
    passed = exact(leave_p, before)
    meet = q_state.astype(F32) * enter_p[...]
    meet = jnp.where(
        iota((8, LANE), 0) < 1,
        jnp.sum(jnp.where(top, meet, 0.0), axis=0, keepdims=True),
        jnp.sum(jnp.where(top, 0.0, meet), axis=0, keepdims=True),
    )
    through = jnp.sum(meet * pdec[...], axis=1, keepdims=True)
    grad_p = live_p * (leave_p / dtp - ratep * (passed + through))
    gdtp_ref[...] = grad_p[0:2, :]

    each(24, 32, intra)

    wait_from(8, q, lambda k: copy(gb_all.at[k], gb_all.at[k], ss_gb.at[0], rs_gb.at[k], s, r))
    total = gb_all[0]
    for k in range(1, 8):
        total = total + gb_all[k]
    go_all[r] = total.astype(BF16)
    each(1, 8, lambda d: gr_copy(d).start())

    def part_b(d):
        g = lax.rem(x + d, 4)
        if d:
            for n in range(2):
                half_slice = b_all.at[part_of(g, n)]
                copy(half_slice, half_slice, ss_b.at[0], rs_b.at[2 * g + n], s, r).wait_recv()
        b_g = b_ref[:, lanes(g)]
        wide = pl.ds(pl.multiple_of(g * ROWS, ROWS), ROWS)

        def pair(j):
            i = g * PER + j
            pulled = mm_nt(b_g, b_all[lanes(i), :])
            inter = wx[:, lanes(i)] * pulled
            xd = x_ref[:, lanes(i)].astype(F32) * inter
            gain = jnp.where(left, skip_ref[2 * i], skip_ref[2 * i + 1])
            grad = dxi[:, lanes(i)] + inter + gain * cot[:, lanes(i)].astype(F32)
            gx_ref[:, lanes(i)] = grad.astype(BF16)
            collect(i, -xd, xd)
            leave = jnp.sum(xd, axis=0, keepdims=True)
            row = iota((8, LANE), 0)
            slot = 2 * lax.rem(i, 4) + (iota((8, LANE), 1) >= 64).astype(jnp.int32)
            at8 = pl.ds(pl.multiple_of(i // 4 * 8, 8), 8)
            car[at8, :] = car[at8, :] + jnp.where(row == slot, leave, 0.0)

        each(0, PER, pair, 2)
        grad_b = mm_tn(pooled[g].astype(BF16), c_ref[:, lanes(g)]) + mm(xw[:, wide], b_all[wide, :])
        gb_ref[:, lanes(g)] = grad_b.astype(BF16)
        pltpu.make_async_copy(gx_ref.at[:, wide], gx_hbm.at[:, wide], out_sem.at[d]).start()

    def part_e(d):
        g = lax.rem(x + d, 4)
        if d:
            for n in range(2):
                half_slice = e_all.at[part_of(g, n)]
                copy(half_slice, half_slice, ss_e.at[0], rs_e.at[2 * g + n], s, r).wait_recv()
        c_g = c_ref[:, lanes(g)]
        wide = pl.ds(pl.multiple_of(g * ROWS, ROWS), ROWS)

        def pair(j):
            i = g * PER + j
            entry = e_all[lanes(i), :]
            seen = mm_nt(c_g, entry)
            z_hi, z_lo = halves(cw[:, lanes(i)].astype(F32) * seen)
            lane = iota((8, 2 * LANE), 1)
            slot = 2 * lax.rem(i, 4) + (lax.rem(lane, LANE) >= 64).astype(jnp.int32)
            pick = (iota((8, 2 * LANE), 0) == slot).astype(F32).astype(BF16)
            at8 = pl.ds(pl.multiple_of(i // 4 * 8, 8), 8)
            zs[at8, :] = zs[at8, :] + mm_nt(pick, jnp.concatenate([z_hi, z_lo], axis=1))
            prod = entry.astype(F32) * b_all[lanes(i), :].astype(F32)
            row = iota((8, LANE), 0)
            here = 2 * lax.rem(i, 4)
            one = jnp.sum(jnp.where(top, prod, 0.0), axis=0, keepdims=True) * decay[pl.ds(2 * i, 1), :]
            two = jnp.sum(jnp.where(top, 0.0, prod), axis=0, keepdims=True) * decay[pl.ds(2 * i + 1, 1), :]
            add = jnp.where(row == here, one, 0.0) + jnp.where(row == here + 1, two, 0.0)
            car[at8, :] = car[at8, :] + add

        each(0, PER, pair, 2)
        grad_c = mm(pooled[g].astype(BF16), b_ref[:, lanes(g)]) + mm(cw[:, wide], e_all[wide, :])
        gc_ref[:, lanes(g)] = grad_c.astype(BF16)

    part_b(0)

    @pl.when(z == 1)
    def _():
        wait_from(4, x, lambda k: copy(l_all.at[k], l_all.at[k], ss_l.at[0], rs_l.at[k], s, r))

        def enter(h):
            rows = head_rows(h)
            state = t_in[rows, :].astype(F32)
            for k in range(4):
                e_out[k, rows, :] = state.astype(BF16)
                if k < 3:
                    state = dec_all[4 + k, pl.ds(h, 1), :] * state + l_all[k, rows, :].astype(F32)

        for n in range(2):
            z_copy(n).wait_recv()
            each(8 * n, 8 * n + 8, enter, 2)
            give_back(e_out, e_all, e_copy, n)

    wait_from(8, q, lambda k: copy(go_all.at[0], go_all.at[y * 8 + k], ss_gr.at[0], rs_gr.at[k], s, r))
    each(1, 4, lambda d: gy_copy(d).start())
    part_b(1)
    part_b(3)
    part_b(2)

    part_e(0)
    part_e(1)
    part_e(3)
    part_e(2)
    carried = jnp.sum(car[...], axis=1, keepdims=True)
    onward = (iota((TOK, TOK), 0) >= iota((TOK, TOK), 1)).astype(F32)
    grad_log = exact(zs[...], onward) + carried
    gdt_ref[...] = live * (xs[...] / dt_ref[...] - rates[...] * grad_log)

    def y_wait(k):
        block = go_all.at[pl.ds(pl.multiple_of(k * 8, 8), 8)]
        copy(block, block, ss_gy.at[0], rs_gy.at[k], s, r).wait_recv()

    each(1, 4, lambda d: y_wait(lax.rem(y + d, 4)))
    for k in range(32):
        gbp_ref[(k % 8) * 32 : (k % 8) * 32 + 32, (k // 8) * LANE : (k // 8 + 1) * LANE] = go_all[k]
    stores = [
        pltpu.make_async_copy(src, dst, out_sem.at[4 + n])
        for n, (src, dst) in enumerate(
            (
                (gxp_ref, gxp_hbm), (gbp_ref, gbp_hbm), (gdtp_ref, gdtp_hbm), (gb_ref, gb_hbm), (gc_ref, gc_hbm),
                (gdt_ref, gdt_hbm),
            )
        )
    ]
    for store in stores:
        store.start()

    each(1, 8, lambda d: d_copy(d).wait_send())
    for make in (p_copy, pd_copy, l_copy):
        each(1, 4, lambda d: make(d).wait_send())
    for n in range(2):
        for make in (b_copy, e_copy):
            each(1, 4, lambda d: make(d, n).wait_send())
        z_copy(n).wait_send()
        h_copy(n).wait_send()
    k_copy().wait_send()
    each(1, 8, lambda d: gb_copy(d).wait_send())
    each(1, 8, lambda d: gr_copy(d).wait_send())
    each(1, 4, lambda d: gy_copy(d).wait_send())
    each(1, 16, lambda d: g_copy(d).wait_send())

    @pl.when(z == 0)
    def _():
        each(1, 4, lambda d: fr_copy(d).wait_send())
        fc_copy().wait_send()

    @pl.when((z == 0) & (y == x))
    def _():
        each(1, 4, lambda d: fy_copy(d).wait_send())

    def q_sent(k):
        @pl.when(jnp.logical_not((k == s) & (y == x)))
        def _():
            q_copy(k).wait_send()

    each(0, 8, q_sent)
    for d in range(4):
        wide = pl.ds(pl.multiple_of(lax.rem(x + d, 4) * ROWS, ROWS), ROWS)
        pltpu.make_async_copy(gx_ref.at[:, wide], gx_hbm.at[:, wide], out_sem.at[d]).wait()
    for store in stores:
        store.wait()


def hand_on(*refs):
    count = (len(refs) - 1) // 2
    moves = [pltpu.make_async_copy(refs[n], refs[count + n], refs[-1].at[n]) for n in range(count)]
    for move in moves:
        move.start()
    for move in moves:
        move.wait()


def local(
    x_prompt, dt_prompt, b_prompt, x_roll, dt_roll, b_roll, c_roll, rate, skip, grad_y, roll_len, prompt_len
):
    anywhere = pl.BlockSpec(memory_space=pl.ANY)
    smem = pl.BlockSpec(memory_space=pltpu.SMEM)
    V = pltpu.VMEM
    dma = pltpu.SemaphoreType.DMA
    wide = HEADS * 64
    ins = (x_prompt, dt_prompt, b_prompt, x_roll[0], dt_roll[0], b_roll[0], c_roll[0], grad_y[0])
    outs = (
        jax.ShapeDtypeStruct((PTOK, LANE), BF16),
        jax.ShapeDtypeStruct((PTOK, 512), BF16),
        jax.ShapeDtypeStruct((2, PTOK), F32),
        jax.ShapeDtypeStruct((TOK, wide), BF16),
        jax.ShapeDtypeStruct((TOK, 512), BF16),
        jax.ShapeDtypeStruct((TOK, 512), BF16),
        jax.ShapeDtypeStruct((HEADS, TOK), F32),
    )
    out = pl.pallas_call(
        kernel,
        name="mixer_backward",
        out_shape=outs,
        in_specs=[anywhere] * 8 + [smem] * 4,
        out_specs=(anywhere,) * 7,
        scratch_shapes=[V(value.shape, value.dtype) for value in ins + outs]
        + [
            V((HEADS, LANE), F32), V((HEADS, TOK), F32), V((HEADS, TOK), F32), V((HEADS, TOK), F32), V((HEADS, LANE), F32),
            V((TOK, wide), BF16), V((TOK, wide), BF16), V((TOK, wide), BF16), V((TOK, wide), F32),
            V((GROUPS, TOK, TOK), F32), V((GROUPS, TOK, TOK), F32), V((TOK, wide), F32),
            V((HEADS, TOK), F32), V((HEADS, TOK), F32), V((HEADS, LANE), F32),
            V((wide, LANE), BF16), V((wide, LANE), BF16), V((4, ROWS, LANE), BF16), V((4, ROWS, LANE), BF16),
            V((8, 16, LANE), F32), V((ROWS, LANE), BF16), V((ROWS, LANE), BF16),
            V((4, ROWS, LANE), BF16), V((4, ROWS, LANE), BF16), V((wide, LANE), BF16), V((wide, LANE), BF16),
            V((4, LANE, LANE), BF16), V((8, LANE), F32), V((4, 8, LANE), F32),
            V((LANE, LANE), BF16), V((LANE, LANE), BF16), V((8, LANE), F32), V((8, LANE), F32),
            V((2, 4, LANE, LANE), BF16), V((LANE, LANE), F32), V((PTOK, LANE), BF16), V((PTOK, LANE), F32),
            V((2, ROWS // 2, LANE), BF16), V((ROWS // 2, LANE), BF16), V((ROWS // 2, LANE), BF16),
            V((16, 32, LANE), BF16), V((32, LANE), F32), V((8, 32, LANE), F32),
            V((PTOK, LANE), F32), V((8, 32, LANE), F32), V((32, 32, LANE), BF16),
            dma((8,)), dma((10,)), dma((4,)), dma((4,)), dma((4,)), dma((4,)), dma((8,)), dma((8,)),
            dma((4,)), dma((4,)), dma((4,)), dma((4,)), dma((2,)), dma((2,)),
            dma((2,)), dma((2,)), dma((4,)), dma((4,)), dma((4,)), dma, dma, dma, dma,
            dma((8,)), dma((8,)), dma((8,)), dma((8,)), dma((16,)), dma((16,)),
            dma((8,)), dma((8,)), dma((8,)), dma((8,)), dma((8,)), dma((8,)), dma((4,)), dma((4,)),
        ],
        compiler_params=pltpu.CompilerParams(
            collective_id=0, has_side_effects=True, vmem_limit_bytes=60 * 1024 * 1024
        ),
        cost_estimate=pl.CostEstimate(flops=1_500_000_000, bytes_accessed=6_000_000, transcendentals=2_000_000),
    )(*ins, rate, skip, roll_len, prompt_len)
    out = pl.pallas_call(
        hand_on,
        name="hand_on",
        out_shape=outs,
        in_specs=[pl.BlockSpec(memory_space=pltpu.VMEM)] * 7,
        out_specs=(anywhere,) * 7,
        scratch_shapes=[dma((7,))],
    )(*out)
    gxp, gbp, gdtp, gx, gb, gc, gdt = out
    return gxp, gbp, gdtp, gx[None], gb[None], gc[None], gdt[None]


def solution(mesh):
    in_specs = (
        P("seq", "roll"), P("roll", "seq"), P("seq", None), P("roll", "seq", None), P("roll", None, "seq"),
        P("roll", "seq", None), P("roll", "seq", None), P(), P(), P("roll", "seq", None), P("roll"), P(),
    )
    out_specs = (
        P("seq", "roll"), P("seq", None), P("roll", "seq"), P("roll", "seq", None), P("roll", "seq", None),
        P("roll", "seq", None), P("roll", None, "seq"),
    )
    return jax.shard_map(local, mesh=mesh, in_specs=in_specs, out_specs=out_specs, check_vma=False)
```

```python
import functools

import jax
import jax.numpy as jnp
from jax import lax
from jax.experimental import pallas as pl
from jax.experimental.pallas import tpu as pltpu
from jax.sharding import PartitionSpec as P

MESH = pl.DeviceIdType.MESH
F32 = jnp.float32
BF16 = jnp.bfloat16
HEADS = 64
GROUPS = 4
TOK = 128
PTOK = 256
LANE = 128
PAIRS = 32
PER = 8
ROWS = 1024
EXACT = lax.Precision.HIGHEST


def iota(shape, axis):
    return lax.broadcasted_iota(jnp.int32, shape, axis)


def mm(a, b):
    return lax.dot_general(a, b, (((1,), (0,)), ((), ())), preferred_element_type=F32)


def mm_nt(a, b):
    return lax.dot_general(a, b, (((1,), (1,)), ((), ())), preferred_element_type=F32)


def mm_tn(a, b):
    return lax.dot_general(a, b, (((0,), (0,)), ((), ())), preferred_element_type=F32)


def exact(a, b):
    return lax.dot_general(a, b, (((1,), (0,)), ((), ())), preferred_element_type=F32, precision=EXACT)


def halves(value):
    high = value.astype(BF16)
    return high, (value - high.astype(F32)).astype(BF16)


def columns(first, second, rows, length):
    stacked = jnp.where(iota((rows, length), 0) < 64, first, second)
    return stacked.T


def each(first, last, act, unroll=1):
    def body(n, carry):
        for k in range(unroll):
            act(first + n * unroll + k)
        return carry

    lax.fori_loop(0, (last - first) // unroll, body, 0)


def kernel(
    xp_hbm, dtp_hbm, bp_hbm, x_hbm, dt_hbm, b_hbm, c_hbm, gy_hbm, rate_ref, skip_ref, len_ref, plen_ref,
    gxp_hbm, gbp_hbm, gdtp_hbm, gx_hbm, gb_hbm, gc_hbm, gdt_hbm,
    xp_ref, dtp_ref, bp_ref, x_ref, dt_ref, b_ref, c_ref, gy_ref,
    gxp_ref, gbp_ref, gdtp_ref, gx_ref, gb_ref, gc_ref, gdt_ref,
    rates, cum, wrow, step, decay, cot, xw, cw, wx, cb, pooled, dxi, zs, xs, car,
    s_loc, l_loc, s_all, l_all, dec_all, t_out, t_in, e_out, b_out, e_all, b_all,
    p_all, pdec, pdec_all, half_out, half_in, hdec_out, hdec_in, fork_all, enter_p, xw_p, wx_p,
    back, sib_in, fg_pieces, fg_all, fg_out, q_all, gbo, gb_all, go_all,
    in_sem, out_sem, ss_p, rs_p, ss_pd, rs_pd, ss_d, rs_d, ss_s, rs_s, ss_l, rs_l, ss_z, rs_z,
    ss_h, rs_h, ss_fy, ss_fr, rs_f, ss_fc, rs_fc, ss_k, rs_k, ss_b, rs_b, ss_e, rs_e, ss_g, rs_g, ss_q, rs_q, ss_gb, rs_gb, ss_gr, rs_gr, ss_gy, rs_gy,
):
    s = lax.axis_index("seq")
    r = lax.axis_index("roll")
    z, x = s // 4, s % 4
    y, q = r // 8, r % 8
    deep, core = q // 2, q % 2
    sibling = r + 1 - 2 * core

    loads = [
        pltpu.make_async_copy(src, dst, in_sem.at[n])
        for n, (src, dst) in enumerate(
            (
                (dt_hbm, dt_ref), (gy_hbm, gy_ref), (c_hbm, c_ref), (dtp_hbm, dtp_ref), (xp_hbm, xp_ref),
                (bp_hbm, bp_ref), (x_hbm, x_ref), (b_hbm, b_ref),
            )
        )
    ]
    for load in loads:
        load.start()

    def at(seq, roll):
        return {"seq": seq, "roll": roll}

    def copy(src, dst, send, recv, seq, roll):
        return pltpu.make_async_remote_copy(
            src_ref=src, dst_ref=dst, send_sem=send, recv_sem=recv, device_id=at(seq, roll), device_id_type=MESH
        )

    bar = pltpu.get_barrier_semaphore()

    def greet(seq, roll):
        pl.semaphore_signal(bar, inc=1, device_id=at(seq, roll), device_id_type=MESH)

    def greet_quarter(k):
        @pl.when(jnp.logical_not((s == k // 4 * 4 + y) & (y == k % 4)))
        def _():
            greet(k // 4 * 4 + y, k % 4 * 8 + q)

    each(1, 8, lambda d: greet(lax.rem(s + d, 8), r))
    each(1, 32, lambda d: greet(s, lax.rem(r + d, 32)))
    each(0, 8, greet_quarter)

    for j in range(HEADS // 8):
        rows8 = jnp.full((8, LANE), rate_ref[8 * j], F32)
        for k in range(1, 8):
            rows8 = jnp.where(iota((8, LANE), 0) == k, rate_ref[8 * j + k], rows8)
        rates[8 * j : 8 * j + 8, :] = rows8
    live = (s * TOK + iota((1, TOK), 1) < len_ref[0]).astype(F32)
    loads[0].wait()
    step[...] = dt_ref[...] * live
    logd = -rates[...] * step[...]
    upto = (iota((TOK, TOK), 0) <= iota((TOK, TOK), 1)).astype(F32)
    cum_v = exact(logd, upto)
    end_v = exact(logd, jnp.ones((TOK, TOK), F32))
    cum[...] = cum_v
    decay[...] = jnp.exp(end_v)
    wrow[...] = step[...] * jnp.exp(end_v - cum_v)

    def slice_of(k):
        return pl.ds(pl.multiple_of(k * ROWS, ROWS), ROWS)

    def lanes(i):
        return pl.ds(pl.multiple_of(i * LANE, LANE), LANE)

    def p_copy(d):
        return copy(p_all.at[x], p_all.at[x], ss_p.at[d], rs_p.at[x], z * 4 + lax.rem(x + d, 4), r)

    def pd_copy(d):
        return copy(pdec, pdec_all.at[x], ss_pd.at[d], rs_pd.at[x], z * 4 + lax.rem(x + d, 4), r)

    def h_copy(n):
        out, there = ((half_out, half_in), (hdec_out, hdec_in))[n]
        return copy(out, there, ss_h.at[n], rs_h.at[n], (1 - z) * 4 + x, r)

    def d_copy(d):
        to = lax.rem(s + d, 8)
        part = pl.ds(pl.multiple_of(to % 4 * 16, 16), 16)
        return copy(decay.at[part], dec_all.at[s], ss_d.at[d], rs_d.at[s], to, r)

    def s_copy(d):
        k = lax.rem(x + d, 4)
        return copy(s_loc.at[slice_of(k)], s_all.at[x], ss_s.at[d], rs_s.at[x], z * 4 + k, r)

    def l_copy(d):
        k = lax.rem(x + d, 4)
        return copy(l_loc.at[slice_of(k)], l_all.at[x], ss_l.at[d], rs_l.at[x], z * 4 + k, r)

    def z_copy(n):
        part = pl.ds(n * (ROWS // 2), ROWS // 2)
        return copy(t_out.at[part], t_in.at[part], ss_z.at[n], rs_z.at[n], (1 - z) * 4 + x, r)

    def fy_copy(d):
        mine = fork_all.at[core, deep]
        return copy(mine, mine, ss_fy.at[d], rs_f.at[deep], s, lax.rem(r + 8 * d, 32))

    def fr_copy(d):
        mine = fork_all.at[core, deep]
        return copy(mine, mine, ss_fr.at[d], rs_f.at[deep], s, y * 8 + lax.rem(deep + d, 4) * 2 + core)

    def fc_copy():
        return copy(fork_all.at[core], fork_all.at[core], ss_fc, rs_fc, s, sibling)

    def part_of(k, n):
        return pl.ds(pl.multiple_of(k * ROWS + n * (ROWS // 2), ROWS // 2), ROWS // 2)

    def b_copy(d, n):
        k = lax.rem(x + d, 4)
        src = b_out.at[k, pl.ds(n * (ROWS // 2), ROWS // 2)]
        return copy(src, b_all.at[part_of(x, n)], ss_b.at[2 * d + n], rs_b.at[2 * x + n], z * 4 + k, r)

    def e_copy(d, n):
        k = lax.rem(x + d, 4)
        src = e_out.at[k, pl.ds(n * (ROWS // 2), ROWS // 2)]
        return copy(src, e_all.at[part_of(x, n)], ss_e.at[2 * d + n], rs_e.at[2 * x + n], z * 4 + k, r)

    def k_copy():
        return copy(back.at[1 - core], sib_in, ss_k, rs_k, s, sibling)

    mine = y * 4 + deep

    def g_copy(d):
        t = lax.rem(mine + d, 16)
        piece = pl.ds(pl.multiple_of(lax.rem(t, 4) * 128 + t // 4 * 32, 32), 32)
        return copy(
            fg_pieces.at[piece], fg_all.at[mine], ss_g.at[d], rs_g.at[mine], s, t // 4 * 8 + lax.rem(t, 4) * 2 + core
        )

    def q_copy(k):
        return copy(fg_out, q_all.at[z * 4 + y], ss_q.at[k], rs_q.at[z * 4 + y], k, x * 8 + q)

    def gb_copy(d):
        t = lax.rem(q + d, 8)
        return copy(gbo.at[pl.ds(pl.multiple_of(t * 32, 32), 32)], gb_all.at[q], ss_gb.at[d], rs_gb.at[q], s, y * 8 + t)

    def gr_copy(d):
        return copy(go_all.at[r], go_all.at[r], ss_gr.at[d], rs_gr.at[q], s, y * 8 + lax.rem(q + d, 8))

    def gy_copy(d):
        block = go_all.at[pl.ds(pl.multiple_of(y * 8, 8), 8)]
        return copy(block, block, ss_gy.at[d], rs_gy.at[y], s, lax.rem(r + 8 * d, 32))

    def wait_from(count, mine, make):
        each(1, count, lambda d: make(lax.rem(mine + d, count)).wait_recv())

    row_live = iota((TOK, LANE), 0) + s * TOK < len_ref[0]
    left = iota((TOK, LANE), 1) < 64
    top = iota((LANE, LANE), 0) < 64
    zero = jnp.zeros((LANE, LANE), F32)

    def s_pair(i, c_g):
        cx = columns(cum[pl.ds(2 * i, 1), :], cum[pl.ds(2 * i + 1, 1), :], LANE, TOK)
        ct = jnp.where(row_live, gy_ref[:, lanes(i)].astype(F32), 0.0)
        cot[:, lanes(i)] = ct.astype(BF16)
        weighted = (ct * jnp.exp(cx)).astype(BF16)
        cw[:, lanes(i)] = weighted
        s_loc[lanes(i), :] = mm_tn(weighted, c_g).astype(BF16)

    def l_pair(i, b_g):
        wide = columns(wrow[pl.ds(2 * i, 1), :], wrow[pl.ds(2 * i + 1, 1), :], LANE, TOK)
        wx[:, lanes(i)] = wide
        weighted = (x_ref[:, lanes(i)].astype(F32) * wide).astype(BF16)
        xw[:, lanes(i)] = weighted
        l_loc[lanes(i), :] = mm_tn(weighted, b_g).astype(BF16)

    loads[1].wait()
    loads[2].wait()
    def summarize(d):
        g = lax.rem(x + d, 4)
        c_g = c_ref[:, lanes(g)]
        each(0, PER, lambda i: s_pair(g * PER + i, c_g), 4)

    summarize(2)
    pl.semaphore_wait(bar, 46 - (y == x).astype(jnp.int32))
    s_copy(2).start()
    each(1, 8, lambda d: d_copy(d).start())
    dec_all[s] = decay[pl.ds(pl.multiple_of(x * 16, 16), 16), :]

    for n in (3, 4, 5):
        loads[n].wait()
    low8 = iota((8, PTOK), 0) < 1
    dtp = jnp.where(low8, dtp_ref[0:1, :], dtp_ref[1:2, :])
    ratep = jnp.where(low8, rate_ref[2 * r], rate_ref[2 * r + 1])
    first_live = 8 * PTOK - plen_ref[0]
    live_p = (s * PTOK + iota((1, PTOK), 1) >= first_live).astype(F32)
    step_p = dtp * live_p
    logd_p = -ratep * step_p
    upto_p = (iota((PTOK, PTOK), 0) <= iota((PTOK, PTOK), 1)).astype(F32)
    cum_p = exact(logd_p, upto_p)
    end_p = exact(logd_p, jnp.ones((PTOK, PTOK), F32))
    w_p = step_p * jnp.exp(end_p - cum_p)
    pdec[...] = jnp.exp(end_p[:, 0:LANE])
    wx_p[...] = columns(w_p[0:1, :], w_p[1:2, :], LANE, PTOK)
    xw_p[...] = (xp_ref[...].astype(F32) * wx_p[...]).astype(BF16)
    bp = bp_ref[:, lanes(y)]
    p_all[x] = mm_tn(xw_p[...], bp).astype(BF16)
    pdec_all[x] = pdec[...]
    each(1, 4, lambda d: p_copy(d).start())
    each(1, 4, lambda d: pd_copy(d).start())

    for d in (1, 3):
        summarize(d)
        s_copy(d).start()
    summarize(0)
    s_all[x] = s_loc[slice_of(x), :]

    loads[6].wait()
    loads[7].wait()
    for g in range(GROUPS):
        b_g = b_ref[:, g * LANE : (g + 1) * LANE]
        each(0, PER, lambda i: l_pair(g * PER + i, b_g), 4)
    l_all[x] = l_loc[slice_of(x), :]

    wait_from(4, x, lambda k: copy(p_all.at[k], p_all.at[k], ss_p.at[0], rs_p.at[k], s, r))
    wait_from(4, x, lambda k: copy(pdec, pdec_all.at[k], ss_pd.at[0], rs_pd.at[k], s, r))

    def pdecay(ref):
        return jnp.where(top, ref[0:1, :], ref[1:2, :])

    half = p_all[0].astype(F32)
    hdec = pdec_all[0]
    for k in range(1, 4):
        half = pdecay(pdec_all.at[k]) * half + p_all[k].astype(F32)
        hdec = hdec * pdec_all[k]
    half_out[...] = half.astype(BF16)
    hdec_out[...] = hdec
    h_copy(0).start()
    h_copy(1).start()

    for g in range(GROUPS):
        cb[g] = mm_nt(c_ref[:, g * LANE : (g + 1) * LANE], b_ref[:, g * LANE : (g + 1) * LANE])
        pooled[g] = zero
    zs[...] = jnp.zeros_like(zs)
    xs[...] = jnp.zeros_like(xs)
    car[...] = jnp.zeros_like(car)
    causal = iota((TOK, TOK), 0) >= iota((TOK, TOK), 1)

    def collect(i, zz, xd):
        z_hi, z_lo = halves(zz)
        row = iota((16, 3 * LANE), 0)
        lane = iota((16, 3 * LANE), 1)
        slot = 2 * lax.rem(i, 4) + (lax.rem(lane, LANE) >= 64).astype(jnp.int32)
        slot = slot + jnp.where(lane >= 2 * LANE, 8, 0)
        pick = (row == slot).astype(F32).astype(BF16)
        sums = mm_nt(pick, jnp.concatenate([z_hi, z_lo, xd.astype(BF16)], axis=1))
        at8 = pl.ds(pl.multiple_of(i // 4 * 8, 8), 8)
        zs[at8, :] = zs[at8, :] + sums[0:8]
        xs[at8, :] = xs[at8, :] + sums[8:16]

    def intra(i):
        g = i // PER
        xi = x_ref[:, lanes(i)]
        ci = cot[:, lanes(i)]
        xf = xi.astype(F32)
        cf = ci.astype(F32)
        both = jnp.concatenate([jnp.where(left, cf, 0.0).astype(BF16), jnp.where(left, 0.0, cf).astype(BF16)], axis=0)
        gx = mm_nt(both, xi)
        cbg = cb[g]
        mixes = []
        total = pooled[g]
        for a in range(2):
            row = cum[pl.ds(2 * i + a, 1), :]
            col = jnp.broadcast_to(row, (TOK, TOK)).T
            seg = jnp.where(causal, jnp.exp(col - row), 0.0) * step[pl.ds(2 * i + a, 1), :]
            total = total + seg * gx[a * TOK : (a + 1) * TOK]
            mixes.append((seg * cbg).astype(BF16))
        pooled[g] = total
        mix = jnp.concatenate(mixes, axis=0)
        dx = mm_tn(mix, both)
        yy = mm(mix, xi)
        yi = jnp.where(left, yy[:TOK], yy[TOK:])
        dxi[:, lanes(i)] = dx
        xd = xf * dx
        collect(i, cf * yi - xd, xd)

    each(0, 6, intra)

    each(1, 4, lambda d: s_copy(d).wait_send())
    for d in (2, 1, 3):
        l_copy(d).start()

    h_copy(0).wait_recv()
    h_copy(1).wait_recv()
    enter_p[...] = jnp.where(z == 1, half_in[...].astype(F32), 0.0)
    for k in range(3):
        moved = pdecay(pdec_all.at[k]) * enter_p[...] + p_all[k].astype(F32)
        enter_p[...] = jnp.where(k < x, moved, enter_p[...])

    @pl.when((z == 0) & (y == x))
    def _():
        fork_all[core, deep] = (pdecay(hdec_in) * half + half_in[...].astype(F32)).astype(BF16)
        each(1, 4, lambda d: fy_copy(d).start())
        each(1, 4, lambda d: fr_copy(d).start())

    def fork_slot(k):
        slot = fork_all.at[core, k]
        return copy(slot, slot, ss_fr.at[0], rs_f.at[k], s, r)

    wait_from(8, s, lambda k: copy(decay.at[pl.ds(0, 16)], dec_all.at[k], ss_d.at[0], rs_d.at[k], s, r))
    wait_from(4, x, lambda k: copy(s_all.at[k], s_all.at[k], ss_s.at[0], rs_s.at[k], s, r))

    def head_rows(h):
        return pl.ds(pl.multiple_of(h * 64, 64), 64)

    def give_back(out, whole, make, n):
        for d in (2, 1, 3):
            make(d, n).start()
        whole[part_of(x, n), :] = out[x, n * (ROWS // 2) : (n + 1) * (ROWS // 2), :]

    def keep_back(h, state):
        rows = pl.ds(pl.multiple_of(h // 4 * 128 + lax.rem(h, 2) * 64, 64), 64)
        back[lax.rem(h // 2, 2), rows, :] = state.astype(BF16)

    @pl.when(z == 1)
    def _():
        def body(h):
            rows = head_rows(h)
            state = jnp.zeros((64, LANE), F32)
            for k in (3, 2, 1, 0):
                b_out[k, rows, :] = state.astype(BF16)
                state = dec_all[4 + k, pl.ds(h, 1), :] * state + s_all[k, rows, :].astype(F32)
            t_out[rows, :] = state.astype(BF16)
            for k in range(4):
                state = dec_all[k, pl.ds(h, 1), :] * state
            keep_back(h, state)

        for n in range(2):
            each(8 * n, 8 * n + 8, body, 2)
            z_copy(n).start()
        k_copy().start()

    @pl.when(z == 0)
    def _():
        def body(h):
            rows = head_rows(h)
            state = s_all[3, rows, :].astype(F32)
            for k in (2, 1, 0):
                state = dec_all[k, pl.ds(h, 1), :] * state + s_all[k, rows, :].astype(F32)
            keep_back(h, state)

        each(0, 16, body, 2)
        k_copy().start()

    @pl.when((z == 0) & (y != x))
    def _():
        fork_slot(deep).wait_recv()
        each(1, 4, lambda d: fr_copy(d).start())

    each(6, 8, intra)

    k_copy().wait_recv()
    fg_pieces[...] = (back[core].astype(F32) + sib_in[...].astype(F32)).astype(BF16)
    each(1, 16, lambda d: g_copy(d).start())
    fg_all[mine] = fg_pieces[pl.ds(pl.multiple_of(deep * 128 + y * 32, 32), 32), :]

    @pl.when(z == 0)
    def _():
        wait_from(4, deep, fork_slot)
        fc_copy().start()

    each(8, 14, intra)

    wait_from(16, mine, lambda k: copy(fg_all.at[k], fg_all.at[k], ss_g.at[0], rs_g.at[k], s, r))
    total = fg_all[0].astype(F32)
    for k in range(1, 16):
        total = total + fg_all[k].astype(F32)
    fg_out[...] = total

    def q_send(k):
        @pl.when(jnp.logical_not((k == s) & (y == x)))
        def _():
            q_copy(k).start()

    each(0, 8, q_send)

    @pl.when(y == x)
    def _():
        q_all[z * 4 + y] = total

    def leave(h):
        rows = head_rows(h)
        state = t_in[rows, :].astype(F32)
        for k in (3, 2, 1, 0):
            b_out[k, rows, :] = state.astype(BF16)
            if k:
                state = dec_all[k, pl.ds(h, 1), :] * state + s_all[k, rows, :].astype(F32)

    def leave_half(n):
        z_copy(n).wait_recv()
        each(8 * n, 8 * n + 8, leave, 2)
        give_back(b_out, b_all, b_copy, n)

    @pl.when(z == 1)
    def _():
        for n in range(2):
            give_back(b_out, b_all, b_copy, n)

    @pl.when(z == 0)
    def _():
        leave_half(0)

    @pl.when(z == 0)
    def _():
        wait_from(4, x, lambda k: copy(l_all.at[k], l_all.at[k], ss_l.at[0], rs_l.at[k], s, r))
        copy(fork_all.at[0], fork_all.at[1 - core], ss_fc, rs_fc, s, r).wait_recv()

        def enter(h):
            rows = head_rows(h)
            first = pl.ds(pl.multiple_of(lax.rem(h, 2) * 64, 64), 64)
            state = fork_all[lax.rem(h // 2, 2), h // 4, first, :].astype(F32)
            for k in range(4):
                e_out[k, rows, :] = state.astype(BF16)
                state = dec_all[k, pl.ds(h, 1), :] * state + l_all[k, rows, :].astype(F32)
            t_out[rows, :] = state.astype(BF16)

        for n in range(2):
            each(8 * n, 8 * n + 8, enter, 2)
            z_copy(n).start()
        leave_half(1)
        for n in range(2):
            give_back(e_out, e_all, e_copy, n)

    each(14, 24, intra)

    def q_wait(k):
        @pl.when(jnp.logical_not((s == k // 4 * 4 + y) & (y == k % 4)))
        def _():
            copy(fg_out, q_all.at[k], ss_q.at[0], rs_q.at[k], s, r).wait_recv()

    each(0, 8, q_wait)
    q_whole = jnp.concatenate([q_all[k] + q_all[4 + k] for k in range(4)], axis=0)
    q_whole = q_whole * jnp.where(z == 0, pdecay(hdec_in), 1.0)
    for k in range(1, 4):
        q_whole = q_whole * jnp.where(k > x, pdecay(pdec_all.at[k]), 1.0)
    q_state = q_whole.astype(BF16)
    pulled_p = mm_nt(bp, q_state)
    dx_p = wx_p[...] * pulled_p
    gxp_ref[...] = dx_p.astype(BF16)
    gbo[...] = mm(xw_p[...], q_state)
    each(1, 8, lambda d: gb_copy(d).start())
    gb_all[q] = gbo[pl.ds(pl.multiple_of(q * 32, 32), 32), :]
    xd_p = xp_ref[...].astype(F32) * dx_p
    xd_hi, xd_lo = halves(xd_p)
    pick = (iota((8, 2 * LANE), 0) == (lax.rem(iota((8, 2 * LANE), 1), LANE) >= 64).astype(jnp.int32)).astype(F32)
    leave_p = mm_nt(pick.astype(BF16), jnp.concatenate([xd_hi, xd_lo], axis=1))
    before = (iota((PTOK, PTOK), 0) < iota((PTOK, PTOK), 1)).astype(F32)
    passed = exact(leave_p, before)
    meet = q_state.astype(F32) * enter_p[...]
    meet = jnp.where(
        iota((8, LANE), 0) < 1,
        jnp.sum(jnp.where(top, meet, 0.0), axis=0, keepdims=True),
        jnp.sum(jnp.where(top, 0.0, meet), axis=0, keepdims=True),
    )
    through = jnp.sum(meet * pdec[...], axis=1, keepdims=True)
    grad_p = live_p * (leave_p / dtp - ratep * (passed + through))
    gdtp_ref[...] = grad_p[0:2, :]

    each(24, 32, intra)

    wait_from(8, q, lambda k: copy(gb_all.at[k], gb_all.at[k], ss_gb.at[0], rs_gb.at[k], s, r))
    total = gb_all[0]
    for k in range(1, 8):
        total = total + gb_all[k]
    go_all[r] = total.astype(BF16)
    each(1, 8, lambda d: gr_copy(d).start())

    def part_b(d, n):
        g = lax.rem(x + d, 4)
        if d:
            half_slice = b_all.at[part_of(g, n)]
            copy(half_slice, half_slice, ss_b.at[0], rs_b.at[2 * g + n], s, r).wait_recv()
        b_g = b_ref[:, lanes(g)]
        wide = pl.ds(pl.multiple_of(g * ROWS, ROWS), ROWS)

        def pair(j):
            i = g * PER + j
            pulled = mm_nt(b_g, b_all[lanes(i), :])
            inter = wx[:, lanes(i)] * pulled
            xd = x_ref[:, lanes(i)].astype(F32) * inter
            gain = jnp.where(left, skip_ref[2 * i], skip_ref[2 * i + 1])
            grad = dxi[:, lanes(i)] + inter + gain * cot[:, lanes(i)].astype(F32)
            gx_ref[:, lanes(i)] = grad.astype(BF16)
            collect(i, -xd, xd)
            leave = jnp.sum(xd, axis=0, keepdims=True)
            row = iota((8, LANE), 0)
            slot = 2 * lax.rem(i, 4) + (iota((8, LANE), 1) >= 64).astype(jnp.int32)
            at8 = pl.ds(pl.multiple_of(i // 4 * 8, 8), 8)
            car[at8, :] = car[at8, :] + jnp.where(row == slot, leave, 0.0)

        each(n * PER // 2, (n + 1) * PER // 2, pair, 4)
        if n == 0:
            return
        grad_b = mm_tn(pooled[g].astype(BF16), c_ref[:, lanes(g)]) + mm(xw[:, wide], b_all[wide, :])
        gb_ref[:, lanes(g)] = grad_b.astype(BF16)
        pltpu.make_async_copy(gx_ref.at[:, wide], gx_hbm.at[:, wide], out_sem.at[d]).start()

    def part_e(d, n):
        g = lax.rem(x + d, 4)
        if d:
            half_slice = e_all.at[part_of(g, n)]
            copy(half_slice, half_slice, ss_e.at[0], rs_e.at[2 * g + n], s, r).wait_recv()
        c_g = c_ref[:, lanes(g)]
        wide = pl.ds(pl.multiple_of(g * ROWS, ROWS), ROWS)

        def pair(j):
            i = g * PER + j
            entry = e_all[lanes(i), :]
            seen = mm_nt(c_g, entry)
            z_hi, z_lo = halves(cw[:, lanes(i)].astype(F32) * seen)
            lane = iota((8, 2 * LANE), 1)
            slot = 2 * lax.rem(i, 4) + (lax.rem(lane, LANE) >= 64).astype(jnp.int32)
            pick = (iota((8, 2 * LANE), 0) == slot).astype(F32).astype(BF16)
            at8 = pl.ds(pl.multiple_of(i // 4 * 8, 8), 8)
            zs[at8, :] = zs[at8, :] + mm_nt(pick, jnp.concatenate([z_hi, z_lo], axis=1))
            prod = entry.astype(F32) * b_all[lanes(i), :].astype(F32)
            row = iota((8, LANE), 0)
            here = 2 * lax.rem(i, 4)
            one = jnp.sum(jnp.where(top, prod, 0.0), axis=0, keepdims=True) * decay[pl.ds(2 * i, 1), :]
            two = jnp.sum(jnp.where(top, 0.0, prod), axis=0, keepdims=True) * decay[pl.ds(2 * i + 1, 1), :]
            add = jnp.where(row == here, one, 0.0) + jnp.where(row == here + 1, two, 0.0)
            car[at8, :] = car[at8, :] + add

        each(n * PER // 2, (n + 1) * PER // 2, pair, 4)
        if n == 0:
            return
        grad_c = mm(pooled[g].astype(BF16), b_ref[:, lanes(g)]) + mm(cw[:, wide], e_all[wide, :])
        gc_ref[:, lanes(g)] = grad_c.astype(BF16)

    part_b(0, 0)
    part_b(0, 1)

    @pl.when(z == 1)
    def _():
        wait_from(4, x, lambda k: copy(l_all.at[k], l_all.at[k], ss_l.at[0], rs_l.at[k], s, r))

        def enter(h):
            rows = head_rows(h)
            state = t_in[rows, :].astype(F32)
            for k in range(4):
                e_out[k, rows, :] = state.astype(BF16)
                if k < 3:
                    state = dec_all[4 + k, pl.ds(h, 1), :] * state + l_all[k, rows, :].astype(F32)

        for n in range(2):
            z_copy(n).wait_recv()
            each(8 * n, 8 * n + 8, enter, 2)
            give_back(e_out, e_all, e_copy, n)

    wait_from(8, q, lambda k: copy(go_all.at[0], go_all.at[y * 8 + k], ss_gr.at[0], rs_gr.at[k], s, r))
    each(1, 4, lambda d: gy_copy(d).start())
    for n in range(2):
        for d in (1, 3, 2):
            part_b(d, n)

    part_e(0, 0)
    part_e(0, 1)
    for n in range(2):
        for d in (1, 3, 2):
            part_e(d, n)
    carried = jnp.sum(car[...], axis=1, keepdims=True)
    onward = (iota((TOK, TOK), 0) >= iota((TOK, TOK), 1)).astype(F32)
    grad_log = exact(zs[...], onward) + carried
    gdt_ref[...] = live * (xs[...] / dt_ref[...] - rates[...] * grad_log)

    def y_wait(k):
        block = go_all.at[pl.ds(pl.multiple_of(k * 8, 8), 8)]
        copy(block, block, ss_gy.at[0], rs_gy.at[k], s, r).wait_recv()

    each(1, 4, lambda d: y_wait(lax.rem(y + d, 4)))
    for k in range(32):
        gbp_ref[(k % 8) * 32 : (k % 8) * 32 + 32, (k // 8) * LANE : (k // 8 + 1) * LANE] = go_all[k]
    stores = [
        pltpu.make_async_copy(src, dst, out_sem.at[4 + n])
        for n, (src, dst) in enumerate(
            (
                (gxp_ref, gxp_hbm), (gbp_ref, gbp_hbm), (gdtp_ref, gdtp_hbm), (gb_ref, gb_hbm), (gc_ref, gc_hbm),
                (gdt_ref, gdt_hbm),
            )
        )
    ]
    for store in stores:
        store.start()

    each(1, 8, lambda d: d_copy(d).wait_send())
    for make in (p_copy, pd_copy, l_copy):
        each(1, 4, lambda d: make(d).wait_send())
    for n in range(2):
        for make in (b_copy, e_copy):
            each(1, 4, lambda d: make(d, n).wait_send())
        z_copy(n).wait_send()
        h_copy(n).wait_send()
    k_copy().wait_send()
    each(1, 8, lambda d: gb_copy(d).wait_send())
    each(1, 8, lambda d: gr_copy(d).wait_send())
    each(1, 4, lambda d: gy_copy(d).wait_send())
    each(1, 16, lambda d: g_copy(d).wait_send())

    @pl.when(z == 0)
    def _():
        each(1, 4, lambda d: fr_copy(d).wait_send())
        fc_copy().wait_send()

    @pl.when((z == 0) & (y == x))
    def _():
        each(1, 4, lambda d: fy_copy(d).wait_send())

    def q_sent(k):
        @pl.when(jnp.logical_not((k == s) & (y == x)))
        def _():
            q_copy(k).wait_send()

    each(0, 8, q_sent)
    for d in range(4):
        wide = pl.ds(pl.multiple_of(lax.rem(x + d, 4) * ROWS, ROWS), ROWS)
        pltpu.make_async_copy(gx_ref.at[:, wide], gx_hbm.at[:, wide], out_sem.at[d]).wait()
    for store in stores:
        store.wait()


def hand_on(*refs):
    count = (len(refs) - 1) // 2
    moves = [pltpu.make_async_copy(refs[n], refs[count + n], refs[-1].at[n]) for n in range(count)]
    for move in moves:
        move.start()
    for move in moves:
        move.wait()


def local(
    x_prompt, dt_prompt, b_prompt, x_roll, dt_roll, b_roll, c_roll, rate, skip, grad_y, roll_len, prompt_len
):
    anywhere = pl.BlockSpec(memory_space=pl.ANY)
    smem = pl.BlockSpec(memory_space=pltpu.SMEM)
    V = pltpu.VMEM
    dma = pltpu.SemaphoreType.DMA
    wide = HEADS * 64
    ins = (x_prompt, dt_prompt, b_prompt, x_roll[0], dt_roll[0], b_roll[0], c_roll[0], grad_y[0])
    outs = (
        jax.ShapeDtypeStruct((PTOK, LANE), BF16),
        jax.ShapeDtypeStruct((PTOK, 512), BF16),
        jax.ShapeDtypeStruct((2, PTOK), F32),
        jax.ShapeDtypeStruct((TOK, wide), BF16),
        jax.ShapeDtypeStruct((TOK, 512), BF16),
        jax.ShapeDtypeStruct((TOK, 512), BF16),
        jax.ShapeDtypeStruct((HEADS, TOK), F32),
    )
    out = pl.pallas_call(
        kernel,
        name="mixer_backward",
        out_shape=outs,
        in_specs=[anywhere] * 8 + [smem] * 4,
        out_specs=(anywhere,) * 7,
        scratch_shapes=[V(value.shape, value.dtype) for value in ins + outs]
        + [
            V((HEADS, LANE), F32), V((HEADS, TOK), F32), V((HEADS, TOK), F32), V((HEADS, TOK), F32), V((HEADS, LANE), F32),
            V((TOK, wide), BF16), V((TOK, wide), BF16), V((TOK, wide), BF16), V((TOK, wide), F32),
            V((GROUPS, TOK, TOK), F32), V((GROUPS, TOK, TOK), F32), V((TOK, wide), F32),
            V((HEADS, TOK), F32), V((HEADS, TOK), F32), V((HEADS, LANE), F32),
            V((wide, LANE), BF16), V((wide, LANE), BF16), V((4, ROWS, LANE), BF16), V((4, ROWS, LANE), BF16),
            V((8, 16, LANE), F32), V((ROWS, LANE), BF16), V((ROWS, LANE), BF16),
            V((4, ROWS, LANE), BF16), V((4, ROWS, LANE), BF16), V((wide, LANE), BF16), V((wide, LANE), BF16),
            V((4, LANE, LANE), BF16), V((8, LANE), F32), V((4, 8, LANE), F32),
            V((LANE, LANE), BF16), V((LANE, LANE), BF16), V((8, LANE), F32), V((8, LANE), F32),
            V((2, 4, LANE, LANE), BF16), V((LANE, LANE), F32), V((PTOK, LANE), BF16), V((PTOK, LANE), F32),
            V((2, ROWS // 2, LANE), BF16), V((ROWS // 2, LANE), BF16), V((ROWS // 2, LANE), BF16),
            V((16, 32, LANE), BF16), V((32, LANE), F32), V((8, 32, LANE), F32),
            V((PTOK, LANE), F32), V((8, 32, LANE), F32), V((32, 32, LANE), BF16),
            dma((8,)), dma((10,)), dma((4,)), dma((4,)), dma((4,)), dma((4,)), dma((8,)), dma((8,)),
            dma((4,)), dma((4,)), dma((4,)), dma((4,)), dma((2,)), dma((2,)),
            dma((2,)), dma((2,)), dma((4,)), dma((4,)), dma((4,)), dma, dma, dma, dma,
            dma((8,)), dma((8,)), dma((8,)), dma((8,)), dma((16,)), dma((16,)),
            dma((8,)), dma((8,)), dma((8,)), dma((8,)), dma((8,)), dma((8,)), dma((4,)), dma((4,)),
        ],
        compiler_params=pltpu.CompilerParams(
            collective_id=0, has_side_effects=True, vmem_limit_bytes=60 * 1024 * 1024
        ),
        cost_estimate=pl.CostEstimate(flops=1_500_000_000, bytes_accessed=6_000_000, transcendentals=2_000_000),
    )(*ins, rate, skip, roll_len, prompt_len)
    out = pl.pallas_call(
        hand_on,
        name="hand_on",
        out_shape=outs,
        in_specs=[pl.BlockSpec(memory_space=pltpu.VMEM)] * 7,
        out_specs=(anywhere,) * 7,
        scratch_shapes=[dma((7,))],
    )(*out)
    gxp, gbp, gdtp, gx, gb, gc, gdt = out
    return gxp, gbp, gdtp, gx[None], gb[None], gc[None], gdt[None]


def solution(mesh):
    in_specs = (
        P("seq", "roll"), P("roll", "seq"), P("seq", None), P("roll", "seq", None), P("roll", None, "seq"),
        P("roll", "seq", None), P("roll", "seq", None), P(), P(), P("roll", "seq", None), P("roll"), P(),
    )
    out_specs = (
        P("seq", "roll"), P("seq", None), P("roll", "seq"), P("roll", "seq", None), P("roll", "seq", None),
        P("roll", "seq", None), P("roll", None, "seq"),
    )
    return jax.shard_map(local, mesh=mesh, in_specs=in_specs, out_specs=out_specs, check_vma=False)
```
